256 devices in a mesh: dp: 2 (over core), fsdp: 128 (over z, x, y).
Axes of the slice: x: 4, y: 4, z: 8, core: 2. Of those that a mesh axis runs over, the one named last changes fastest.
Arguments:
- grad_parts: bfloat16 [2, 128, 262144], P('dp', None, 'fsdp'), may hold values from -0.29882812 to 0.29882812
- held_block: int32 [128], replicated, may hold values from 0 to 127, each once
- refresh: int32 [16], replicated, may hold values from 0 to 127, as said below
- left_prev: float32 [128, 512, 512], P('fsdp'), as said below
- right_prev: float32 [128, 512, 512], P('fsdp'), as said below
- left_root_prev: float32 [128, 512, 512], P('fsdp'), as said below
- right_root_prev: float32 [128, 512, 512], P('fsdp'), as said below
Outputs:
- update: bfloat16 [128, 262144], P(None, 'fsdp')
- left_factor: float32 [128, 512, 512], P('fsdp')
- right_factor: float32 [128, 512, 512], P('fsdp')
- left_root: float32 [128, 512, 512], P('fsdp')
- right_root: float32 [128, 512, 512], P('fsdp')
The draws below stay inside these ranges and needn't reach their ends.
Inputs may be any that keep to these rules, and one draw needn't show every extreme that they name: `held_block`: each block id appears exactly once. `refresh`: 16 distinct block ids. `left_prev`: symmetric with a positive diagonal larger than the sum of magnitudes of the rest of its row. `right_prev`: symmetric with a positive diagonal larger than the sum of magnitudes of the rest of its row. `left_root_prev`: symmetric. `right_root_prev`: symmetric.
All inputs are finite; a program needn't handle non-finite values.
Results may differ from the reference program's by a relative error of at most 0.012.
Values may be sent and summed in bfloat16 or wider, within the bound.
No kernel may reach another device: no remote copies, remote signals or barrier semaphores. Data moves between devices by JAX's collectives and lax.ppermute only.
A program may use at most 64 MiB of HBM per device.

```python
import math
import jax
import jax.numpy as jnp
from jax import lax

BLK = 512
ITERS = 2
NB = 128
NR = 16
N_DP = 2


def dominant_block(key, low, high):
    key_off, key_diag = jax.random.split(key)
    off_noise = jax.random.uniform(key_off, (NB, BLK, BLK), jnp.float32, -1.0, 1.0) / BLK
    symmetric = (off_noise + jnp.swapaxes(off_noise, 1, 2)) * 0.5
    diagonal_vals = 1.5 + jnp.exp(jax.random.uniform(key_diag, (NB, BLK), jnp.float32, math.log(low), math.log(high)))
    identity = jnp.eye(BLK, dtype=jnp.float32)
    return symmetric * (1.0 - identity) + identity * diagonal_vals[:, :, None]


def root_block(key, low, high):
    key_off, key_diag = jax.random.split(key)
    off_noise = jax.random.normal(key_off, (NB, BLK, BLK), jnp.float32) * (0.3 / math.sqrt(BLK))
    symmetric = (off_noise + jnp.swapaxes(off_noise, 1, 2)) * 0.7
    diagonal_vals = jnp.exp(jax.random.uniform(key_diag, (NB, BLK), jnp.float32, math.log(low), math.log(high)))
    identity = jnp.eye(BLK, dtype=jnp.float32)
    return symmetric * (1.0 - identity) + identity * diagonal_vals[:, :, None]


def draw_refresh(key, part):
    key = jax.random.fold_in(key, 11)
    key_perm, key_slot = jax.random.split(key)
    chosen = jax.random.permutation(key_perm, NB)[:NR].astype(jnp.int32)
    slot_pick = jax.random.randint(key_slot, (), 0, NR)
    chosen = jnp.where(jnp.any(chosen == NB - 1), chosen, chosen.at[slot_pick].set(NB - 1))
    return chosen.astype(jnp.int32)


def draw_left_prev(key, part):
    key = jax.random.fold_in(key, 21)
    return dominant_block(key, 0.5, 5.0)


def draw_right_prev(key, part):
    key = jax.random.fold_in(key, 31)
    return dominant_block(key, 0.5, 5.0)


def draw_left_root_prev(key, part):
    key = jax.random.fold_in(key, 41)
    return root_block(key, 0.2, 1.0)


def draw_right_root_prev(key, part):
    key = jax.random.fold_in(key, 51)
    return root_block(key, 0.2, 1.0)


def block_scale(key, extent, shards, least, largest):
    loudness, own = 1.0, jax.random.fold_in(key, 6)
    for position, blocks in shards:
        steps = jnp.exp(jax.random.uniform(jax.random.fold_in(own, position), (blocks,), jnp.float32, least / len(shards), largest / len(shards)))
        loudness = loudness * jnp.repeat(steps, extent[position] // blocks).reshape([-1 if axis == position else 1 for axis in range(len(extent))])
    return loudness


def gaussian(own_key, extent, width, limit, cuts=(), held_as=jnp.bfloat16):
    result = jax.random.normal(own_key, extent, jnp.float32) * width
    if len(cuts) > 0:
        result = block_scale(own_key, extent, cuts, -0.22, 0.18) * result
    return jnp.clip(result, min=-limit, max=limit).astype(held_as)


def setup_inputs(seed: int = 0) -> dict:
    arg_keys = jax.random.split(jax.random.key(seed), 8)
    return {
        "grad_parts": gaussian(arg_keys[0], (N_DP, NB, BLK * BLK), 0.05, 0.29882812, ((0, 2), (2, 128))),
        "held_block": jax.random.permutation(arg_keys[1], NB).astype(jnp.int32),
        "refresh": draw_refresh(jax.random.fold_in(arg_keys[7], 71), 0),
        "left_prev": draw_left_prev(jax.random.fold_in(arg_keys[7], 71), 0),
        "right_prev": draw_right_prev(jax.random.fold_in(arg_keys[7], 71), 0),
        "left_root_prev": draw_left_root_prev(jax.random.fold_in(arg_keys[7], 71), 0),
        "right_root_prev": draw_right_root_prev(jax.random.fold_in(arg_keys[7], 71), 0),
    }


shift_eps = 0.001

def matmul_high(left, right):
    return jnp.dot(left, right, precision=lax.Precision.HIGHEST, preferred_element_type=jnp.float32)

def newton_root(matrix):
    identity = jnp.eye(BLK, dtype=jnp.float32)
    shifted = matrix + shift_eps * identity
    trace_scale = jnp.trace(shifted) / BLK
    current = shifted / trace_scale
    iterate = identity * trace_scale ** (-0.25)
    for iteration in range(ITERS):
        newton_step = (5.0 * identity - current) * 0.25
        iterate = matmul_high(iterate, newton_step)
        squared = matmul_high(newton_step, newton_step)
        fourth_power = matmul_high(squared, squared)
        current = matmul_high(fourth_power, current)
    return iterate

def reference(grad_parts, held_block, refresh, left_prev, right_prev, left_root_prev, right_root_prev):
    summed = lax.optimization_barrier(jnp.sum(grad_parts.astype(jnp.float32), axis=0))
    gradient = summed[held_block].reshape(NB, BLK, BLK)
    refresh_flag = jnp.any(held_block[:, None] == refresh[None, :], axis=1)

    def per_slot(slot_items):
        grad_block, flag_now, left_old, right_old, left_keep, right_keep = slot_items
        rounded = grad_block.astype(jnp.bfloat16)
        left_new = left_old + jnp.dot(rounded, rounded.T, preferred_element_type=jnp.float32)
        right_new = right_old + jnp.dot(rounded.T, rounded, preferred_element_type=jnp.float32)
        left_use, right_use = lax.cond(flag_now, lambda: (newton_root(left_new), newton_root(right_new)), lambda: (left_keep, right_keep))
        raw = matmul_high(matmul_high(left_use, grad_block), right_use)
        graft = raw * jnp.sqrt(jnp.sum(grad_block * grad_block)) / jnp.sqrt(jnp.sum(raw * raw) + 1e-06)
        return (graft, left_new, right_new, left_use, right_use)
    graft, left_factor, right_factor, left_root, right_root = lax.map(per_slot, (gradient, refresh_flag, left_prev, right_prev, left_root_prev, right_root_prev))
    update = jnp.zeros((NB, BLK * BLK), jnp.float32).at[held_block].set(graft.reshape(NB, BLK * BLK))
    return (update.astype(jnp.bfloat16), left_factor, right_factor, left_root, right_root)
```

```python
import functools

import jax
import jax.numpy as jnp
from jax import lax
from jax.experimental import pallas as pl
from jax.experimental.pallas import tpu as pltpu
from jax.sharding import PartitionSpec as P

BLK = 512
NB = 128
ROWS = 8
EPS = 0.001
F32 = jnp.float32
BF16 = jnp.bfloat16
VMEM_LIMIT = 24 * 1024 * 1024


def one_hot(held):
    block = lax.broadcasted_iota(jnp.int32, (NB, NB), 0)
    return jnp.where(block == held, 1.0, 0.0).astype(BF16)


def send_order_kernel(held_ref, mine_ref, theirs_ref, out_ref, rows_ref):
    half = lax.axis_index("dp")
    placed = one_hot(held_ref[...])
    for part in range(ROWS):
        columns = pl.ds(pl.multiple_of(half * (ROWS * 128) + part * 128, 128), 128)
        summed = (mine_ref[:, columns].astype(F32) + theirs_ref[:, columns].astype(F32)).astype(BF16)
        ordered = lax.dot_general(placed, summed, (((0,), (0,)), ((), ())), preferred_element_type=F32)
        rows_ref[pl.ds(part, NB, stride=ROWS), :] = ordered
    out_ref[...] = rows_ref[...].astype(BF16)


def restore_kernel(held_ref, mine_ref, theirs_ref, out_ref, rows_ref):
    half = lax.axis_index("dp")
    placed = one_hot(held_ref[...])
    for ref, which in ((mine_ref, half), (theirs_ref, 1 - half)):
        rows_ref[...] = ref[...].astype(F32)
        for part in range(ROWS):
            columns = pl.ds(pl.multiple_of(which * (ROWS * 128) + part * 128, 128), 128)
            piece = rows_ref[pl.ds(part, NB, stride=ROWS), :].astype(BF16)
            out_ref[:, columns] = jnp.dot(placed, piece, preferred_element_type=F32).astype(BF16)


def split(value):
    high = value.astype(BF16)
    return high, (value - high.astype(F32)).astype(BF16)


def store_left(ref, rows, value):
    high, low = split(value)
    ref[rows, 0:BLK] = high
    ref[rows, BLK : 2 * BLK] = high
    ref[rows, 2 * BLK : 3 * BLK] = low


def store_right(ref, row, count, value):
    high, low = split(value)
    ref[pl.ds(row, count), :] = high
    ref[pl.ds(BLK + row, count), :] = low
    ref[pl.ds(2 * BLK + row, count), :] = high


def product(left_ref, right_ref):
    return jnp.dot(left_ref[...], right_ref[...], preferred_element_type=F32)


CHUNK = 64


def chunks(body):
    for start in range(0, BLK, CHUNK):
        body(start, slice(start, start + CHUNK))


def newton(factor_ref, root_ref, left_ref, right_ref, scaled_ref, prod_ref):
    def eye(start):
        row = lax.broadcasted_iota(jnp.int32, (CHUNK, BLK), 0) + start
        return row == lax.broadcasted_iota(jnp.int32, (CHUNK, BLK), 1)

    trace = jnp.full((1, 1), BLK * EPS, F32)
    for start in range(0, BLK, 128):
        block = factor_ref[start : start + 128, start : start + 128]
        row = lax.broadcasted_iota(jnp.int32, (128, 128), 0)
        column = lax.broadcasted_iota(jnp.int32, (128, 128), 1)
        trace = trace + jnp.sum(jnp.where(row == column, block, 0.0), keepdims=True)
    scale = trace * (1.0 / BLK)
    inverse = 1.0 / scale
    fourth = lax.rsqrt(jnp.sqrt(scale))

    def first(start, rows):
        scaled = (factor_ref[rows, :] + jnp.where(eye(start), EPS, 0.0)) * inverse
        scaled_ref[rows, :] = scaled
        store_left(left_ref, rows, scaled)
        store_right(right_ref, start, CHUNK, scaled)

    chunks(first)
    prod_ref[...] = product(left_ref, right_ref)

    def second(start, rows):
        square = (jnp.where(eye(start), 25.0, 0.0) - 10.0 * scaled_ref[rows, :] + prod_ref[rows, :]) * 0.0625
        store_left(left_ref, rows, square)
        store_right(right_ref, start, CHUNK, square)

    chunks(second)
    root_ref[...] = product(left_ref, right_ref)

    def third(start, rows):
        store_left(left_ref, rows, root_ref[rows, :])
        store_right(right_ref, start, CHUNK, (5.0 * scaled_ref[rows, :] - prod_ref[rows, :]) * 0.25)

    chunks(third)
    prod_ref[...] = product(left_ref, right_ref)

    def fourth_root(start, rows):
        step = (jnp.where(eye(start), 5.0, 0.0) - scaled_ref[rows, :]) * 0.25
        root_ref[rows, :] = (1.25 * step - 0.25 * prod_ref[rows, :]) * fourth

    chunks(fourth_root)


def owner_kernel(
    mine_ref, theirs_ref, held_hbm, refresh_hbm, left_prev, right_prev, left_root_prev, right_root_prev,
    out_ref, left_out, right_out, left_root_out, right_root_out,
    flat_ref, grad_ref, left_f, right_f, left_r, right_r, left3, right3, scaled_ref, prod_ref,
    held_ref, refresh_ref, in_sems, out_sems,
):
    half = lax.axis_index("dp")
    slot = lax.axis_index("fsdp")
    loads = [
        pltpu.make_async_copy(source, target, in_sems.at[i])
        for i, (source, target) in enumerate(
            (
                (left_prev, left_f),
                (right_prev, right_f),
                (held_hbm, held_ref),
                (refresh_hbm, refresh_ref),
                (left_root_prev, left_r),
                (right_root_prev, right_r),
            )
        )
    ]
    stores = [
        pltpu.make_async_copy(source, target, out_sems.at[i])
        for i, (source, target) in enumerate(
            ((left_f, left_out), (right_f, right_out), (left_r, left_root_out), (right_r, right_root_out))
        )
    ]
    for load in loads:
        load.start()

    for ref, which in ((mine_ref, half), (theirs_ref, 1 - half)):
        for source in range(NB):
            start = pl.multiple_of(source * 16 + which * ROWS, ROWS)
            flat_ref[pl.ds(start, ROWS), :] = ref[source * ROWS : (source + 1) * ROWS, :].astype(F32)
    total = jnp.zeros((8, 128), F32)
    for quarter in range(4):
        part = flat_ref[pl.ds(quarter, BLK, stride=4), :]
        grad_ref[:, quarter * 128 : (quarter + 1) * 128] = part.astype(BF16)
        total = total + jnp.sum((part * part).reshape(BLK // 8, 8, 128), axis=0)
    grad_norm = jnp.sqrt(jnp.sum(total, keepdims=True))

    grad = grad_ref[...]
    loads[0].wait()
    left_f[...] += lax.dot_general(grad, grad, (((1,), (1,)), ((), ())), preferred_element_type=F32)
    stores[0].start()
    loads[1].wait()
    right_f[...] += lax.dot_general(grad, grad, (((0,), (0,)), ((), ())), preferred_element_type=F32)
    stores[1].start()
    for load in loads[2:]:
        load.wait()

    held = held_ref[slot]
    refreshed = refresh_ref[0] == held
    for i in range(1, refresh_ref.shape[0]):
        refreshed = refreshed | (refresh_ref[i] == held)

    @pl.when(refreshed)
    def _():
        newton(left_f, left_r, left3, right3, scaled_ref, prod_ref)
        newton(right_f, right_r, left3, right3, scaled_ref, prod_ref)

    stores[2].start()
    stores[3].start()

    def split_left(start, rows):
        high, low = split(left_r[rows, :])
        left3[rows, 0:BLK] = high
        left3[rows, BLK : 2 * BLK] = low

    def split_right(start, rows):
        store_right(right3, start, CHUNK, right_r[rows, :])

    chunks(split_left)
    chunks(split_right)
    prod_ref[...] = jnp.dot(left3[:, 0:BLK], grad_ref[...], preferred_element_type=F32) + jnp.dot(
        left3[:, BLK : 2 * BLK], grad_ref[...], preferred_element_type=F32
    )

    def split_product(start, rows):
        store_left(left3, rows, prod_ref[rows, :])

    chunks(split_product)
    prod_ref[...] = product(left3, right3)

    total = jnp.zeros((8, BLK), F32)
    for start in range(0, BLK, CHUNK):
        part = prod_ref[start : start + CHUNK, :]
        total = total + jnp.sum((part * part).reshape(CHUNK // 8, 8, BLK), axis=0)
    graft = grad_norm / jnp.sqrt(jnp.sum(total, keepdims=True) + 1e-06)
    for quarter in range(4):
        flat_ref[pl.ds(quarter, BLK, stride=4), :] = prod_ref[:, quarter * 128 : (quarter + 1) * 128] * graft
    for target in range(NB):
        start = pl.multiple_of(target * 16 + half * ROWS, ROWS)
        out_ref[target * ROWS : (target + 1) * ROWS, :] = flat_ref[pl.ds(start, ROWS), :].astype(BF16)
    for store in stores:
        store.wait()


def vmem():
    return pl.BlockSpec(memory_space=pltpu.VMEM)


def anywhere():
    return pl.BlockSpec(memory_space=pl.ANY)


def params(limit=VMEM_LIMIT):
    return pltpu.CompilerParams(vmem_limit_bytes=limit)


def swap(value):
    return lax.ppermute(value, "dp", [(0, 1), (1, 0)])


def exchange(messages):
    moved = lax.all_to_all(messages.reshape(NB, ROWS, 128), "fsdp", split_axis=0, concat_axis=0, tiled=True)
    return moved.reshape(NB * ROWS, 128)


def local(grad_parts, held_block, refresh, left_prev, right_prev, left_root_prev, right_root_prev):
    mine = grad_parts[0]
    held_row = held_block.reshape(1, NB)
    message = jax.ShapeDtypeStruct((NB * ROWS, 128), BF16)
    matrix = jax.ShapeDtypeStruct((BLK, BLK), F32)

    ordered = pl.pallas_call(
        send_order_kernel,
        out_shape=message,
        in_specs=[vmem()] * 3,
        out_specs=vmem(),
        scratch_shapes=[pltpu.VMEM((NB * ROWS, 128), F32)],
        compiler_params=params(),
        name="send_order",
    )(held_row, mine, swap(mine))
    got = exchange(ordered)

    outgoing, left_new, right_new, left_use, right_use = pl.pallas_call(
        owner_kernel,
        out_shape=(message, matrix, matrix, matrix, matrix),
        in_specs=[vmem()] * 2 + [anywhere()] * 6,
        out_specs=(vmem(), anywhere(), anywhere(), anywhere(), anywhere()),
        scratch_shapes=[
            pltpu.VMEM((2048, 128), F32),
            pltpu.VMEM((BLK, BLK), BF16),
            pltpu.VMEM((BLK, BLK), F32),
            pltpu.VMEM((BLK, BLK), F32),
            pltpu.VMEM((BLK, BLK), F32),
            pltpu.VMEM((BLK, BLK), F32),
            pltpu.VMEM((BLK, 3 * BLK), BF16),
            pltpu.VMEM((3 * BLK, BLK), BF16),
            pltpu.VMEM((BLK, BLK), F32),
            pltpu.VMEM((BLK, BLK), F32),
            pltpu.SMEM((NB,), jnp.int32),
            pltpu.SMEM(refresh.shape, jnp.int32),
            pltpu.SemaphoreType.DMA((6,)),
            pltpu.SemaphoreType.DMA((4,)),
        ],
        compiler_params=params(),
        name="owner",
    )(got, swap(got), held_block, refresh, left_prev[0], right_prev[0], left_root_prev[0], right_root_prev[0])

    back = exchange(outgoing)
    update = pl.pallas_call(
        restore_kernel,
        out_shape=jax.ShapeDtypeStruct((NB, 2048), BF16),
        in_specs=[vmem()] * 3,
        out_specs=vmem(),
        scratch_shapes=[pltpu.VMEM((NB * ROWS, 128), F32)],
        compiler_params=params(),
        name="restore",
    )(held_row, back, swap(back))
    return (update, left_new[None], right_new[None], left_use[None], right_use[None])


def solution(mesh):
    placed = (
        P("dp", None, "fsdp"),
        P(),
        P(),
        P("fsdp", None, None),
        P("fsdp", None, None),
        P("fsdp", None, None),
        P("fsdp", None, None),
    )
    return jax.shard_map(
        local,
        mesh=mesh,
        in_specs=placed,
        out_specs=(
            P(None, "fsdp"),
            P("fsdp", None, None),
            P("fsdp", None, None),
            P("fsdp", None, None),
            P("fsdp", None, None),
        ),
        check_vma=False,
    )
```

```python
import functools

import jax
import jax.numpy as jnp
from jax import lax
from jax.experimental import pallas as pl
from jax.experimental.pallas import tpu as pltpu
from jax.sharding import PartitionSpec as P

BLK = 512
NB = 128
ROWS = 8
EPS = 0.001
F32 = jnp.float32
BF16 = jnp.bfloat16
VMEM_LIMIT = 24 * 1024 * 1024


def one_hot(held):
    block = lax.broadcasted_iota(jnp.int32, (NB, NB), 0)
    return jnp.where(block == held, 1.0, 0.0).astype(BF16)


def to_slots(placed, value):
    return lax.dot_general(placed, value, (((0,), (0,)), ((), ())), preferred_element_type=F32)


def own_order_kernel(held_ref, mine_hbm, rows_ref, mine_ref, sem):
    half = lax.axis_index("dp")
    columns = pl.ds(pl.multiple_of(half * (ROWS * 128), 128), ROWS * 128)
    load = pltpu.make_async_copy(mine_hbm.at[:, columns], mine_ref, sem)
    load.start()
    load.wait()
    placed = one_hot(held_ref[...])
    for part in range(ROWS):
        rows_ref[pl.ds(part, NB, stride=ROWS), :] = to_slots(placed, mine_ref[:, part * 128 : (part + 1) * 128])


def send_order_kernel(held_ref, own_ref, theirs_ref, out_ref, rows_ref):
    half = lax.axis_index("dp")
    placed = one_hot(held_ref[...])
    for part in range(ROWS):
        columns = pl.ds(pl.multiple_of(half * (ROWS * 128) + part * 128, 128), 128)
        rows_ref[pl.ds(part, NB, stride=ROWS), :] = to_slots(placed, theirs_ref[:, columns])
    out_ref[...] = (rows_ref[...] + own_ref[...]).astype(BF16)


def restore_kernel(held_ref, mine_ref, theirs_ref, out_ref, rows_ref):
    half = lax.axis_index("dp")
    placed = one_hot(held_ref[...])
    for ref, which in ((mine_ref, half), (theirs_ref, 1 - half)):
        rows_ref[...] = ref[...].astype(F32)
        for part in range(ROWS):
            columns = pl.ds(pl.multiple_of(which * (ROWS * 128) + part * 128, 128), 128)
            piece = rows_ref[pl.ds(part, NB, stride=ROWS), :].astype(BF16)
            out_ref[:, columns] = jnp.dot(placed, piece, preferred_element_type=F32).astype(BF16)


def split(value):
    high = value.astype(BF16)
    return high, (value - high.astype(F32)).astype(BF16)


def store_split(ref, rows, value):
    ref[0, rows, :], ref[1, rows, :] = split(value)


def product(left_ref, right_ref):
    return (
        jnp.dot(left_ref[0], right_ref[0], preferred_element_type=F32)
        + jnp.dot(left_ref[0], right_ref[1], preferred_element_type=F32)
        + jnp.dot(left_ref[1], right_ref[0], preferred_element_type=F32)
    )


CHUNK = 64


def eye(start):
    row = lax.broadcasted_iota(jnp.int32, (CHUNK, BLK), 0) + start
    return row == lax.broadcasted_iota(jnp.int32, (CHUNK, BLK), 1)


def newton(sides):
    scales = []
    for factor_ref, _, left_ref, _, shift_ref, _ in sides:
        trace = jnp.full((1, 1), BLK * EPS, F32)
        for start in range(0, BLK, 128):
            block = factor_ref[start : start + 128, start : start + 128]
            row = lax.broadcasted_iota(jnp.int32, (128, 128), 0)
            column = lax.broadcasted_iota(jnp.int32, (128, 128), 1)
            trace = trace + jnp.sum(jnp.where(row == column, block, 0.0), keepdims=True)
        scale = trace * (1.0 / BLK)
        inverse = 1.0 / scale
        scales.append(lax.rsqrt(jnp.sqrt(scale)))
        on_diagonal = EPS * inverse - 1.0
        for start in range(0, BLK, CHUNK):
            rows = slice(start, start + CHUNK)
            shifted = factor_ref[rows, :] * inverse + jnp.where(eye(start), on_diagonal, 0.0)
            shift_ref[rows, :] = shifted
            store_split(left_ref, rows, shifted)
    for _, _, left_ref, _, _, prod_ref in sides:
        prod_ref[...] = product(left_ref, left_ref)
    for _, _, left_ref, _, shift_ref, prod_ref in sides:
        for start in range(0, BLK, CHUNK):
            rows = slice(start, start + CHUNK)
            store_split(left_ref, rows, prod_ref[rows, :] * 0.0625 - shift_ref[rows, :] * 0.5)
    for _, root_ref, left_ref, _, _, _ in sides:
        root_ref[...] = product(left_ref, left_ref)
    for _, root_ref, left_ref, right_ref, shift_ref, prod_ref in sides:
        for start in range(0, BLK, CHUNK):
            rows = slice(start, start + CHUNK)
            shifted, square, quartic = shift_ref[rows, :], prod_ref[rows, :], root_ref[rows, :]
            partial = shifted - square * 0.125
            store_split(left_ref, rows, quartic - partial)
            store_split(right_ref, rows, shifted * 0.75 - square * 0.25)
            root_ref[rows, :] = partial + quartic
    for _, _, left_ref, right_ref, _, prod_ref in sides:
        prod_ref[...] = product(left_ref, right_ref)
    for (_, root_ref, _, _, _, prod_ref), scale in zip(sides, scales):
        for start in range(0, BLK, CHUNK):
            rows = slice(start, start + CHUNK)
            total = root_ref[rows, :] + prod_ref[rows, :]
            root_ref[rows, :] = (jnp.where(eye(start), 1.0, 0.0) - total * 0.25) * scale


def owner_kernel(
    mine_ref, theirs_ref, held_hbm, refresh_hbm, left_prev, right_prev, left_root_prev, right_root_prev,
    out_ref, left_out, right_out, left_root_out, right_root_out,
    flat_ref, grad_ref, left_f, right_f, left_r, right_r,
    left_a, left_b, left_n, left_p, right_a, right_b, right_n, right_p,
    held_ref, refresh_ref, in_sems, out_sems,
):
    half = lax.axis_index("dp")
    slot = lax.axis_index("fsdp")
    loads = [
        pltpu.make_async_copy(source, target, in_sems.at[i])
        for i, (source, target) in enumerate(
            (
                (held_hbm, held_ref),
                (refresh_hbm, refresh_ref),
                (left_root_prev, left_r),
                (right_root_prev, right_r),
            )
        )
    ]
    stores = [
        pltpu.make_async_copy(source, target, out_sems.at[i])
        for i, (source, target) in enumerate(
            ((left_f, left_out), (right_f, right_out), (left_r, left_root_out), (right_r, right_root_out))
        )
    ]
    for load in loads:
        load.start()

    for ref, which in ((mine_ref, half), (theirs_ref, 1 - half)):
        for source in range(NB):
            start = pl.multiple_of(source * 16 + which * ROWS, ROWS)
            flat_ref[pl.ds(start, ROWS), :] = ref[source * ROWS : (source + 1) * ROWS, :].astype(F32)
    total = jnp.zeros((8, 128), F32)
    for quarter in range(4):
        part = flat_ref[pl.ds(quarter, BLK, stride=4), :]
        grad_ref[:, quarter * 128 : (quarter + 1) * 128] = part.astype(BF16)
        total = total + jnp.sum((part * part).reshape(BLK // 8, 8, 128), axis=0)
    grad_norm = jnp.sqrt(jnp.sum(total, keepdims=True))

    grad = grad_ref[...]
    left_f[...] = left_prev[...] + lax.dot_general(grad, grad, (((1,), (1,)), ((), ())), preferred_element_type=F32)
    stores[0].start()
    right_f[...] = right_prev[...] + lax.dot_general(grad, grad, (((0,), (0,)), ((), ())), preferred_element_type=F32)
    stores[1].start()
    for load in loads:
        load.wait()

    held = held_ref[slot]
    refreshed = refresh_ref[0] == held
    for i in range(1, refresh_ref.shape[0]):
        refreshed = refreshed | (refresh_ref[i] == held)

    @pl.when(refreshed)
    def _():
        newton(
            (
                (left_f, left_r, left_a, left_b, left_n, left_p),
                (right_f, right_r, right_a, right_b, right_n, right_p),
            )
        )

    stores[2].start()
    stores[3].start()

    for start in range(0, BLK, CHUNK):
        rows = slice(start, start + CHUNK)
        store_split(left_a, rows, left_r[rows, :])
        right_a[0, rows, :] = right_r[rows, :].astype(BF16)
    grad = grad_ref[...]
    half_way = jnp.dot(left_a[0], grad, preferred_element_type=F32) + jnp.dot(
        left_a[1], grad, preferred_element_type=F32
    )
    left_p[...] = jnp.dot(half_way.astype(BF16), right_a[0], preferred_element_type=F32)

    total = jnp.zeros((8, BLK), F32)
    for start in range(0, BLK, CHUNK):
        part = left_p[start : start + CHUNK, :]
        total = total + jnp.sum((part * part).reshape(CHUNK // 8, 8, BLK), axis=0)
    graft = grad_norm / jnp.sqrt(jnp.sum(total, keepdims=True) + 1e-06)
    for quarter in range(4):
        flat_ref[pl.ds(quarter, BLK, stride=4), :] = left_p[:, quarter * 128 : (quarter + 1) * 128] * graft
    for target in range(NB):
        start = pl.multiple_of(target * 16 + half * ROWS, ROWS)
        out_ref[target * ROWS : (target + 1) * ROWS, :] = flat_ref[pl.ds(start, ROWS), :].astype(BF16)
    for store in stores:
        store.wait()


def vmem():
    return pl.BlockSpec(memory_space=pltpu.VMEM)


def hbm():
    return pl.BlockSpec(memory_space=pltpu.HBM)


def stay(value):
    return pltpu.with_memory_space_constraint(value, pltpu.HBM)


def params(limit=VMEM_LIMIT):
    return pltpu.CompilerParams(vmem_limit_bytes=limit)


def swap(value):
    return lax.ppermute(value, "dp", [(0, 1), (1, 0)])


def exchange(messages):
    moved = lax.all_to_all(messages.reshape(NB, ROWS, 128), "fsdp", split_axis=0, concat_axis=0, tiled=True)
    return moved.reshape(NB * ROWS, 128)


def local(grad_parts, held_block, refresh, left_prev, right_prev, left_root_prev, right_root_prev):
    mine = grad_parts[0]
    held_row = held_block.reshape(1, NB)
    message = jax.ShapeDtypeStruct((NB * ROWS, 128), BF16)
    matrix = jax.ShapeDtypeStruct((BLK, BLK), F32)

    theirs = swap(mine)
    own = pl.pallas_call(
        own_order_kernel,
        out_shape=jax.ShapeDtypeStruct((NB * ROWS, 128), F32),
        in_specs=[vmem(), hbm()],
        out_specs=vmem(),
        scratch_shapes=[pltpu.VMEM((NB, ROWS * 128), BF16), pltpu.SemaphoreType.DMA],
        compiler_params=params(),
        cost_estimate=pl.CostEstimate(flops=NB * NB * ROWS * 256, bytes_accessed=8 * NB * ROWS * 128, transcendentals=0),
        name="own_order",
    )(held_row, stay(mine))
    ordered = pl.pallas_call(
        send_order_kernel,
        out_shape=message,
        in_specs=[vmem()] * 3,
        out_specs=vmem(),
        scratch_shapes=[pltpu.VMEM((NB * ROWS, 128), F32)],
        compiler_params=params(),
        name="send_order",
    )(held_row, own, theirs)
    got = exchange(ordered)

    outgoing, left_new, right_new, left_use, right_use = pl.pallas_call(
        owner_kernel,
        out_shape=(message, matrix, matrix, matrix, matrix),
        in_specs=[vmem()] * 2 + [hbm()] * 2 + [vmem()] * 2 + [hbm()] * 2,
        out_specs=(vmem(), hbm(), hbm(), hbm(), hbm()),
        scratch_shapes=[
            pltpu.VMEM((2048, 128), F32),
            pltpu.VMEM((BLK, BLK), BF16),
            pltpu.VMEM((BLK, BLK), F32),
            pltpu.VMEM((BLK, BLK), F32),
            pltpu.VMEM((BLK, BLK), F32),
            pltpu.VMEM((BLK, BLK), F32),
        ]
        + 2
        * [
            pltpu.VMEM((2, BLK, BLK), BF16),
            pltpu.VMEM((2, BLK, BLK), BF16),
            pltpu.VMEM((BLK, BLK), F32),
            pltpu.VMEM((BLK, BLK), F32),
        ]
        + [
            pltpu.SMEM((NB,), jnp.int32),
            pltpu.SMEM(refresh.shape, jnp.int32),
            pltpu.SemaphoreType.DMA((4,)),
            pltpu.SemaphoreType.DMA((4,)),
        ],
        compiler_params=params(),
        name="owner",
    )(got, swap(got), stay(held_block), stay(refresh), left_prev[0], right_prev[0], stay(left_root_prev[0]), stay(right_root_prev[0]))

    back = exchange(outgoing)
    update = pl.pallas_call(
        restore_kernel,
        out_shape=jax.ShapeDtypeStruct((NB, 2048), BF16),
        in_specs=[vmem()] * 3,
        out_specs=vmem(),
        scratch_shapes=[pltpu.VMEM((NB * ROWS, 128), F32)],
        compiler_params=params(),
        name="restore",
    )(held_row, back, swap(back))
    return (update, left_new[None], right_new[None], left_use[None], right_use[None])


def solution(mesh):
    placed = (
        P("dp", None, "fsdp"),
        P(),
        P(),
        P("fsdp", None, None),
        P("fsdp", None, None),
        P("fsdp", None, None),
        P("fsdp", None, None),
    )
    return jax.shard_map(
        local,
        mesh=mesh,
        in_specs=placed,
        out_specs=(
            P(None, "fsdp"),
            P("fsdp", None, None),
            P("fsdp", None, None),
            P("fsdp", None, None),
            P("fsdp", None, None),
        ),
        check_vma=False,
    )
```

```python
import functools

import jax
import jax.numpy as jnp
from jax import lax
from jax.experimental import pallas as pl
from jax.experimental.pallas import tpu as pltpu
from jax.sharding import PartitionSpec as P

BLK = 512
NB = 128
ROWS = 8
EPS = 0.001
F32 = jnp.float32
BF16 = jnp.bfloat16
VMEM_LIMIT = 24 * 1024 * 1024


def one_hot(held):
    block = lax.broadcasted_iota(jnp.int32, (NB, NB), 0)
    return jnp.where(block == held, 1.0, 0.0).astype(BF16)


def to_slots(placed, value):
    return lax.dot_general(placed, value, (((0,), (0,)), ((), ())), preferred_element_type=F32)


def segment_column(part, half):
    return pl.multiple_of((part // 2) * BLK + half * 256 + (part % 2) * 128, 128)


def own_order_kernel(held_ref, mine_hbm, rows_ref, placed_ref, mine_ref, sem):
    half = lax.axis_index("dp")
    load = pltpu.make_async_copy(mine_hbm, mine_ref, sem)
    load.start()
    placed = one_hot(held_ref[...])
    placed_ref[...] = placed
    load.wait()
    for part in range(ROWS):
        columns = pl.ds(segment_column(part, half), 128)
        rows_ref[pl.ds(part, NB, stride=ROWS), :] = to_slots(placed, mine_ref[:, columns])


def send_order_kernel(placed_ref, own_ref, theirs_ref, out_ref, rows_ref):
    half = lax.axis_index("dp")
    placed = placed_ref[...]
    for part in range(ROWS):
        columns = pl.ds(segment_column(part, half), 128)
        rows_ref[pl.ds(part, NB, stride=ROWS), :] = to_slots(placed, theirs_ref[:, columns])
    out_ref[...] = (rows_ref[...] + own_ref[...]).astype(BF16)


def unpack_half(message_ref, rows_ref, write):
    rows_ref[...] = message_ref[...].astype(F32)
    total = jnp.zeros((8, 128), F32)
    for q in range(2):
        part = rows_ref[pl.ds(q, BLK, stride=2), :]
        write(q, part.astype(BF16))
        total = total + jnp.sum((part * part).reshape(BLK // 8, 8, 128), axis=0)
    return total


def own_unpack_kernel(mine_ref, grad_ref, total_ref, rows_ref):
    def write(q, part):
        grad_ref[:, q * 128 : (q + 1) * 128] = part

    total_ref[...] = unpack_half(mine_ref, rows_ref, write)


def restore_half(placed_ref, message_ref, out_hbm, half, rows_ref, whole_ref, sems):
    placed = placed_ref[...]
    rows_ref[...] = message_ref[...].astype(F32)
    copies = []
    for row in range(4):
        for part in (2 * row, 2 * row + 1):
            piece = rows_ref[pl.ds(part, NB, stride=ROWS), :].astype(BF16)
            whole_ref[:, part * 128 : (part + 1) * 128] = jnp.dot(
                placed, piece, preferred_element_type=F32
            ).astype(BF16)
        columns = pl.ds(segment_column(2 * row, half), 256)
        source = whole_ref.at[:, row * 256 : (row + 1) * 256]
        copies.append(pltpu.make_async_copy(source, out_hbm.at[:, columns], sems.at[row]))
        copies[row].start()
    for copy in copies:
        copy.wait()


def own_restore_kernel(placed_ref, mine_ref, out_hbm, rows_ref, whole_ref, sems):
    restore_half(placed_ref, mine_ref, out_hbm, lax.axis_index("dp"), rows_ref, whole_ref, sems)


def restore_kernel(placed_ref, theirs_ref, half_hbm, out_hbm, rows_ref, whole_ref, sems):
    del half_hbm
    restore_half(placed_ref, theirs_ref, out_hbm, 1 - lax.axis_index("dp"), rows_ref, whole_ref, sems)


def split(value):
    high = value.astype(BF16)
    return high, (value - high.astype(F32)).astype(BF16)


def store_split(ref, rows, value):
    ref[0, rows, :], ref[1, rows, :] = split(value)


def store_high(ref, rows, value):
    ref[0, rows, :] = value.astype(BF16)


def product(left_ref, right_ref):
    return (
        product_high(left_ref, right_ref)
        + jnp.dot(left_ref[0], right_ref[1], preferred_element_type=F32)
        + jnp.dot(left_ref[1], right_ref[0], preferred_element_type=F32)
    )


def product_high(left_ref, right_ref):
    return jnp.dot(left_ref[0], right_ref[0], preferred_element_type=F32)


CHUNK = 64


def eye(start):
    row = lax.broadcasted_iota(jnp.int32, (CHUNK, BLK), 0) + start
    return row == lax.broadcasted_iota(jnp.int32, (CHUNK, BLK), 1)


ONE_PASS_ENERGY = 256.0


def newton(sides, store, product, finish):
    scales, energies = [], []

    def shift(factor_ref, root_ref, left_ref, right_ref, shift_ref, prod_ref):
        trace = jnp.full((1, 1), BLK * EPS, F32)
        for start in range(0, BLK, 128):
            block = factor_ref[start : start + 128, start : start + 128]
            row = lax.broadcasted_iota(jnp.int32, (128, 128), 0)
            column = lax.broadcasted_iota(jnp.int32, (128, 128), 1)
            trace = trace + jnp.sum(jnp.where(row == column, block, 0.0), keepdims=True)
        scale = trace * (1.0 / BLK)
        inverse = 1.0 / scale
        scales.append(lax.rsqrt(jnp.sqrt(scale)))
        on_diagonal = EPS * inverse - 1.0
        for start in range(0, BLK, CHUNK):
            rows = slice(start, start + CHUNK)
            shifted = factor_ref[rows, :] * inverse + jnp.where(eye(start), on_diagonal, 0.0)
            shift_ref[rows, :] = shifted
            store(left_ref, rows, shifted)
        prod_ref[...] = product(left_ref, left_ref)

    def square(factor_ref, root_ref, left_ref, right_ref, shift_ref, prod_ref):
        energy = jnp.zeros((8, BLK), F32)
        for start in range(0, BLK, CHUNK):
            rows = slice(start, start + CHUNK)
            value = prod_ref[rows, :]
            energy = energy + jnp.sum((value * value).reshape(CHUNK // 8, 8, BLK), axis=0)
            store(left_ref, rows, value * 0.0625 - shift_ref[rows, :] * 0.5)
        energies.append(jnp.sum(energy, keepdims=True))
        root_ref[...] = product(left_ref, left_ref)

    def quartic(factor_ref, root_ref, left_ref, right_ref, shift_ref, prod_ref):
        for start in range(0, BLK, CHUNK):
            rows = slice(start, start + CHUNK)
            shifted, value = shift_ref[rows, :], prod_ref[rows, :]
            partial, fourth = shifted - value * 0.125, root_ref[rows, :]
            store(left_ref, rows, fourth - partial)
            store(right_ref, rows, shifted * 0.75 - value * 0.25)
            root_ref[rows, :] = partial + fourth
        prod_ref[...] = product(left_ref, right_ref)

    for step in (shift, square, quartic):
        for side in sides:
            step(*side)
    for i, (_, root_ref, _, _, _, prod_ref) in enumerate(sides):
        for start in range(0, BLK, CHUNK):
            rows = slice(start, start + CHUNK)
            total = root_ref[rows, :] + prod_ref[rows, :]
            root_ref[rows, :] = (jnp.where(eye(start), 1.0, 0.0) - total * 0.25) * scales[i]
        finish(i)
    return jnp.maximum(*energies)


def owner_kernel(
    own_ref, own_total_ref, theirs_ref, held_hbm, refresh_hbm, left_prev, right_prev, left_root_prev, right_root_prev,
    out_ref, left_out, right_out, left_root_out, right_root_out,
    rows_ref, grad_ref, left_f, right_f, left_r, right_r, left_kept, right_kept,
    left_a, left_b, left_n, left_p, right_a, right_b, right_n, right_p,
    held_ref, refresh_ref, in_sems, out_sems,
):
    half = lax.axis_index("dp")
    slot = lax.axis_index("fsdp")
    loads = [
        pltpu.make_async_copy(source, target, in_sems.at[i])
        for i, (source, target) in enumerate(
            (
                (held_hbm, held_ref),
                (refresh_hbm, refresh_ref),
                (left_root_prev, left_kept),
                (right_root_prev, right_kept),
            )
        )
    ]
    stores = [
        pltpu.make_async_copy(source, target, out_sems.at[i])
        for i, (source, target) in enumerate(
            ((left_f, left_out), (right_f, right_out), (left_r, left_root_out), (right_r, right_root_out))
        )
    ]
    for load in loads:
        load.start()

    def columns(which, q):
        return pl.ds(pl.multiple_of(which * 256 + q * 128, 128), 128)

    def write(q, part):
        grad_ref[:, columns(1 - half, q)] = part

    total = own_total_ref[...] + unpack_half(theirs_ref, rows_ref, write)
    for q in range(2):
        grad_ref[:, columns(half, q)] = own_ref[:, q * 128 : (q + 1) * 128]
    grad_norm = jnp.sqrt(jnp.sum(total, keepdims=True))

    grad = grad_ref[...]
    left_f[...] = left_prev[...] + lax.dot_general(grad, grad, (((1,), (1,)), ((), ())), preferred_element_type=F32)
    stores[0].start()
    right_f[...] = right_prev[...] + lax.dot_general(grad, grad, (((0,), (0,)), ((), ())), preferred_element_type=F32)
    stores[1].start()
    for load in loads[:2]:
        load.wait()

    held = held_ref[slot]
    refreshed = refresh_ref[0] == held
    for i in range(1, refresh_ref.shape[0]):
        refreshed = refreshed | (refresh_ref[i] == held)

    def split_roots(left, right):
        for start in range(0, BLK, CHUNK):
            rows = slice(start, start + CHUNK)
            store_split(left_a, rows, left[rows, :])
            right_a[0, rows, :] = right[rows, :].astype(BF16)

    @pl.when(refreshed)
    def _():
        sides = (
            (left_f, left_r, left_a, left_b, left_n, left_p),
            (right_f, right_r, right_a, right_b, right_n, right_p),
        )

        def finish(i):
            stores[2 + i].start()

        energy = newton(sides, store_high, product_high, finish)

        @pl.when(jnp.logical_not(energy[0, 0] <= ONE_PASS_ENERGY))
        def _():
            stores[2].wait()
            stores[3].wait()
            newton(sides, store_split, product, finish)

        split_roots(left_r, right_r)
        for load in loads[2:]:
            load.wait()

    @pl.when(jnp.logical_not(refreshed))
    def _():
        for load in loads[2:]:
            load.wait()
        for i, (source, target) in enumerate(((left_kept, left_root_out), (right_kept, right_root_out))):
            pltpu.make_async_copy(source, target, out_sems.at[2 + i]).start()
        split_roots(left_kept, right_kept)

    grad = grad_ref[...]
    half_way = jnp.dot(left_a[0], grad, preferred_element_type=F32) + jnp.dot(
        left_a[1], grad, preferred_element_type=F32
    )
    left_p[...] = jnp.dot(half_way.astype(BF16), right_a[0], preferred_element_type=F32)

    total = jnp.zeros((8, BLK), F32)
    for start in range(0, BLK, CHUNK):
        part = left_p[start : start + CHUNK, :]
        total = total + jnp.sum((part * part).reshape(CHUNK // 8, 8, BLK), axis=0)
    graft = grad_norm / jnp.sqrt(jnp.sum(total, keepdims=True) + 1e-06)
    for q in range(2):
        rows_ref[pl.ds(q, BLK, stride=2), :] = left_p[:, columns(half, q)] * graft
    out_ref[...] = rows_ref[...].astype(BF16)
    for store in stores:
        store.wait()


def vmem():
    return pl.BlockSpec(memory_space=pltpu.VMEM)


def hbm():
    return pl.BlockSpec(memory_space=pltpu.HBM)


def stay(value):
    return pltpu.with_memory_space_constraint(value, pltpu.HBM)


def params(limit=VMEM_LIMIT):
    return pltpu.CompilerParams(vmem_limit_bytes=limit)


def swap(value):
    return lax.ppermute(value, "dp", [(0, 1), (1, 0)])


def exchange(messages):
    moved = lax.all_to_all(messages.reshape(NB, ROWS, 128), "fsdp", split_axis=0, concat_axis=0, tiled=True)
    return moved.reshape(NB * ROWS, 128)


def local(grad_parts, held_block, refresh, left_prev, right_prev, left_root_prev, right_root_prev):
    mine = grad_parts[0]
    held_row = held_block.reshape(1, NB)
    message = jax.ShapeDtypeStruct((NB * ROWS, 128), BF16)
    matrix = jax.ShapeDtypeStruct((BLK, BLK), F32)

    theirs = swap(mine)
    own, placed = pl.pallas_call(
        own_order_kernel,
        out_shape=(jax.ShapeDtypeStruct((NB * ROWS, 128), F32), jax.ShapeDtypeStruct((NB, NB), BF16)),
        in_specs=[vmem(), hbm()],
        out_specs=(vmem(), vmem()),
        scratch_shapes=[pltpu.VMEM((NB, 2048), BF16), pltpu.SemaphoreType.DMA],
        compiler_params=params(),
        cost_estimate=pl.CostEstimate(flops=NB * NB * ROWS * 256, bytes_accessed=8 * NB * ROWS * 128, transcendentals=0),
        name="own_order",
    )(held_row, stay(mine))
    ordered = pl.pallas_call(
        send_order_kernel,
        out_shape=message,
        in_specs=[vmem()] * 3,
        out_specs=vmem(),
        scratch_shapes=[pltpu.VMEM((NB * ROWS, 128), F32)],
        compiler_params=params(),
        name="send_order",
    )(placed, own, theirs)
    got = exchange(ordered)

    theirs = swap(got)
    own, own_total = pl.pallas_call(
        own_unpack_kernel,
        out_shape=(jax.ShapeDtypeStruct((BLK, 256), BF16), jax.ShapeDtypeStruct((8, 128), F32)),
        in_specs=[vmem()],
        out_specs=(vmem(), vmem()),
        scratch_shapes=[pltpu.VMEM((NB * ROWS, 128), F32)],
        compiler_params=params(),
        cost_estimate=pl.CostEstimate(flops=BLK * 1024, bytes_accessed=4 * NB * ROWS * 128, transcendentals=0),
        name="own_unpack",
    )(got)
    outgoing, left_new, right_new, left_use, right_use = pl.pallas_call(
        owner_kernel,
        out_shape=(message, matrix, matrix, matrix, matrix),
        in_specs=[vmem()] * 3 + [hbm()] * 2 + [vmem()] * 2 + [hbm()] * 2,
        out_specs=(vmem(), hbm(), hbm(), hbm(), hbm()),
        scratch_shapes=[
            pltpu.VMEM((NB * ROWS, 128), F32),
            pltpu.VMEM((BLK, BLK), BF16),
        ]
        + 6 * [pltpu.VMEM((BLK, BLK), F32)]
        + 2
        * [
            pltpu.VMEM((2, BLK, BLK), BF16),
            pltpu.VMEM((2, BLK, BLK), BF16),
            pltpu.VMEM((BLK, BLK), F32),
            pltpu.VMEM((BLK, BLK), F32),
        ]
        + [
            pltpu.SMEM((NB,), jnp.int32),
            pltpu.SMEM(refresh.shape, jnp.int32),
            pltpu.SemaphoreType.DMA((4,)),
            pltpu.SemaphoreType.DMA((4,)),
        ],
        compiler_params=params(),
        name="owner",
    )(
        own,
        own_total,
        theirs,
        stay(held_block),
        stay(refresh),
        left_prev[0],
        right_prev[0],
        stay(left_root_prev[0]),
        stay(right_root_prev[0]),
    )

    back = exchange(outgoing)
    theirs = swap(back)
    restored = jax.ShapeDtypeStruct((NB, 2048), BF16)
    restore_scratch = [
        pltpu.VMEM((NB * ROWS, 128), F32),
        pltpu.VMEM((NB, ROWS * 128), BF16),
        pltpu.SemaphoreType.DMA((4,)),
    ]
    halfway = pl.pallas_call(
        own_restore_kernel,
        out_shape=restored,
        in_specs=[vmem()] * 2,
        out_specs=hbm(),
        scratch_shapes=restore_scratch,
        compiler_params=params(),
        cost_estimate=pl.CostEstimate(flops=NB * NB * ROWS * 256, bytes_accessed=4 * NB * ROWS * 128, transcendentals=0),
        name="own_restore",
    )(placed, back)
    update = pl.pallas_call(
        restore_kernel,
        out_shape=restored,
        in_specs=[vmem()] * 2 + [hbm()],
        out_specs=hbm(),
        scratch_shapes=restore_scratch,
        compiler_params=params(),
        input_output_aliases={2: 0},
        name="restore",
    )(placed, theirs, halfway)
    return (update, left_new[None], right_new[None], left_use[None], right_use[None])


def solution(mesh):
    placed = (
        P("dp", None, "fsdp"),
        P(),
        P(),
        P("fsdp", None, None),
        P("fsdp", None, None),
        P("fsdp", None, None),
        P("fsdp", None, None),
    )
    return jax.shard_map(
        local,
        mesh=mesh,
        in_specs=placed,
        out_specs=(
            P(None, "fsdp"),
            P("fsdp", None, None),
            P("fsdp", None, None),
            P("fsdp", None, None),
            P("fsdp", None, None),
        ),
        check_vma=False,
    )
```

```python
import functools

import jax
import jax.numpy as jnp
from jax import lax
from jax.experimental import pallas as pl
from jax.experimental.pallas import tpu as pltpu
from jax.sharding import PartitionSpec as P

BLK = 512
NB = 128
ROWS = 8
EPS = 0.001
F32 = jnp.float32
BF16 = jnp.bfloat16
VMEM_LIMIT = 24 * 1024 * 1024


def one_hot(held):
    block = lax.broadcasted_iota(jnp.int32, (NB, NB), 0)
    return jnp.where(block == held, 1.0, 0.0).astype(BF16)


def to_slots(placed, value):
    return lax.dot_general(placed, value, (((0,), (0,)), ((), ())), preferred_element_type=F32)


def segment_column(part, half):
    return pl.multiple_of((part // 2) * BLK + half * 256 + (part % 2) * 128, 128)


def own_order_kernel(held_ref, mine_hbm, rows_ref, placed_ref, mine_ref, sem):
    half = lax.axis_index("dp")
    load = pltpu.make_async_copy(mine_hbm, mine_ref, sem)
    load.start()
    placed = one_hot(held_ref[...])
    placed_ref[...] = placed
    load.wait()
    for part in range(ROWS):
        columns = pl.ds(segment_column(part, half), 128)
        rows_ref[pl.ds(part, NB, stride=ROWS), :] = to_slots(placed, mine_ref[:, columns])


def send_order_kernel(placed_ref, own_ref, theirs_ref, out_ref, rows_ref):
    half = lax.axis_index("dp")
    placed = placed_ref[...]
    for part in range(ROWS):
        columns = pl.ds(segment_column(part, half), 128)
        rows_ref[pl.ds(part, NB, stride=ROWS), :] = to_slots(placed, theirs_ref[:, columns])
    out_ref[...] = (rows_ref[...] + own_ref[...]).astype(BF16)


def unpack_half(message_ref, rows_ref, write):
    rows_ref[...] = message_ref[...].astype(F32)
    total = jnp.zeros((8, 128), F32)
    for q in range(2):
        part = rows_ref[pl.ds(q, BLK, stride=2), :]
        write(q, part.astype(BF16))
        total = total + jnp.sum((part * part).reshape(BLK // 8, 8, 128), axis=0)
    return total


def own_unpack_kernel(
    mine_ref, left_prev, held_hbm, refresh_hbm, grad_ref, total_ref, left_ref, flag_ref, rows_ref, held_ref, refresh_ref, sems
):
    loads = [
        pltpu.make_async_copy(held_hbm, held_ref, sems.at[0]),
        pltpu.make_async_copy(refresh_hbm, refresh_ref, sems.at[1]),
    ]
    for load in loads:
        load.start()

    def write(q, part):
        grad_ref[:, q * 128 : (q + 1) * 128] = part

    total_ref[...] = unpack_half(mine_ref, rows_ref, write)
    left_ref[...] = left_prev[...] + outer(grad_ref[...])
    for load in loads:
        load.wait()
    held = held_ref[lax.axis_index("fsdp")]
    refreshed = refresh_ref[0] == held
    for i in range(1, refresh_ref.shape[0]):
        refreshed = refreshed | (refresh_ref[i] == held)
    flag_ref[...] = jnp.full(flag_ref.shape, jnp.where(refreshed, 1.0, 0.0), F32)


def outer(value):
    return lax.dot_general(value, value, (((1,), (1,)), ((), ())), preferred_element_type=F32)


def inner(value):
    return lax.dot_general(value, value, (((0,), (0,)), ((), ())), preferred_element_type=F32)


def restore_half(placed_ref, message_ref, out_hbm, half, rows_ref, whole_ref, sems):
    placed = placed_ref[...]
    rows_ref[...] = message_ref[...].astype(F32)
    copies = []
    for row in range(4):
        for part in (2 * row, 2 * row + 1):
            piece = rows_ref[pl.ds(part, NB, stride=ROWS), :].astype(BF16)
            whole_ref[:, part * 128 : (part + 1) * 128] = jnp.dot(
                placed, piece, preferred_element_type=F32
            ).astype(BF16)
        columns = pl.ds(segment_column(2 * row, half), 256)
        source = whole_ref.at[:, row * 256 : (row + 1) * 256]
        copies.append(pltpu.make_async_copy(source, out_hbm.at[:, columns], sems.at[row]))
        copies[row].start()
    for copy in copies:
        copy.wait()


def own_restore_kernel(placed_ref, mine_ref, root_ref, out_hbm, root_hbm, rows_ref, whole_ref, sems, root_sem):
    store = pltpu.make_async_copy(root_ref, root_hbm, root_sem)
    store.start()
    restore_half(placed_ref, mine_ref, out_hbm, lax.axis_index("dp"), rows_ref, whole_ref, sems)
    store.wait()


def restore_kernel(placed_ref, theirs_ref, half_hbm, out_hbm, rows_ref, whole_ref, sems):
    del half_hbm
    restore_half(placed_ref, theirs_ref, out_hbm, 1 - lax.axis_index("dp"), rows_ref, whole_ref, sems)


def split(value):
    high = value.astype(BF16)
    return high, (value - high.astype(F32)).astype(BF16)


def store_split(ref, rows, value):
    ref[0, rows, :], ref[1, rows, :] = split(value)


def store_high(ref, rows, value):
    ref[0, rows, :] = value.astype(BF16)


def product(left_ref, right_ref):
    return (
        product_high(left_ref, right_ref)
        + jnp.dot(left_ref[0], right_ref[1], preferred_element_type=F32)
        + jnp.dot(left_ref[1], right_ref[0], preferred_element_type=F32)
    )


def product_high(left_ref, right_ref):
    return jnp.dot(left_ref[0], right_ref[0], preferred_element_type=F32)


CHUNK = 64


def add_diagonal(start, value, amount):
    block = start // 128 * 128
    row = lax.broadcasted_iota(jnp.int32, (CHUNK, 128), 0) + (start - block)
    column = lax.broadcasted_iota(jnp.int32, (CHUNK, 128), 1)
    touched = value[:, block : block + 128] + jnp.where(row == column, amount, 0.0)
    parts = [value[:, :block], touched, value[:, block + 128 :]]
    return jnp.concatenate([part for part in parts if part.shape[1]], axis=1)


ONE_PASS_ENERGY = 256.0


def newton(sides, store, product, use, finish):
    scales, inverses, energies = [], [], []

    def shifted(i, start):
        return add_diagonal(start, sides[i][0][start : start + CHUNK, :] * inverses[i], EPS * inverses[i] - 1.0)

    def shift(i, factor_ref, x_ref, y_ref, z_ref, part_ref, root_ref):
        trace = jnp.full((1, 1), BLK * EPS, F32)
        for start in range(0, BLK, 128):
            block = factor_ref[start : start + 128, start : start + 128]
            row = lax.broadcasted_iota(jnp.int32, (128, 128), 0)
            column = lax.broadcasted_iota(jnp.int32, (128, 128), 1)
            trace = trace + jnp.sum(jnp.where(row == column, block, 0.0), keepdims=True)
        scale = trace * (1.0 / BLK)
        inverses.append(1.0 / scale)
        scales.append(lax.rsqrt(jnp.sqrt(scale)))
        for start in range(0, BLK, CHUNK):
            store(x_ref, slice(start, start + CHUNK), shifted(i, start))

    def square(i, factor_ref, x_ref, y_ref, z_ref, part_ref, root_ref):
        value = product(x_ref, x_ref)
        energy = jnp.zeros((8, BLK), F32)
        for start in range(0, BLK, CHUNK):
            rows = slice(start, start + CHUNK)
            first, second = shifted(i, start), value[rows, :]
            energy = energy + jnp.sum((second * second).reshape(CHUNK // 8, 8, BLK), axis=0)
            part = first - second * 0.125
            part_ref[rows, :] = part
            store(y_ref, rows, part * -0.5)
            store(z_ref, rows, first * 0.75 - second * 0.25)
        energies.append(jnp.sum(energy, keepdims=True))

    def quartic(i, factor_ref, x_ref, y_ref, z_ref, part_ref, root_ref):
        value = product(y_ref, y_ref)
        for start in range(0, BLK, CHUNK):
            rows = slice(start, start + CHUNK)
            part, fourth = part_ref[rows, :], value[rows, :]
            part_ref[rows, :] = part + fourth
            store(x_ref, rows, fourth - part)

    def last(i, factor_ref, x_ref, y_ref, z_ref, part_ref, root_ref):
        value = product(x_ref, z_ref)
        for start in range(0, BLK, CHUNK):
            rows = slice(start, start + CHUNK)
            root = add_diagonal(start, (part_ref[rows, :] + value[rows, :]) * (scales[i] * -0.25), scales[i])
            root_ref[rows, :] = root
            use(i, rows, root)
        finish(i)

    for step in (shift, square, quartic, last):
        for i, side in enumerate(sides):
            step(i, *side)
    return jnp.maximum(*energies)


def owner_kernel(
    own_ref, own_total_ref, theirs_ref, left_start, right_prev, flag_ref, left_root_prev, right_root_prev,
    out_ref, left_out, right_out, left_root_out, right_r,
    rows_ref, grad_ref, left_f, right_f, left_r,
    left_x, left_y, left_z, left_p, right_x, right_y, right_z, right_p, left_use, right_use, in_sems, out_sems,
):
    half = lax.axis_index("dp")
    stores = [
        pltpu.make_async_copy(source, target, out_sems.at[i])
        for i, (source, target) in enumerate(
            ((left_f, left_out), (right_f, right_out), (left_r, left_root_out))
        )
    ]

    def columns(which, q):
        return pl.ds(pl.multiple_of(which * 256 + q * 128, 128), 128)

    def factors():
        parts = []

        def write(q, part):
            grad_ref[:, columns(1 - half, q)] = part
            parts.append(part)

        total = own_total_ref[...] + unpack_half(theirs_ref, rows_ref, write)
        for q in range(2):
            grad_ref[:, columns(half, q)] = own_ref[:, q * 128 : (q + 1) * 128]
        left_f[...] = left_start[...] + outer(jnp.concatenate(parts, axis=1))
        stores[0].start()
        right_f[...] = right_prev[...] + inner(grad_ref[...])
        stores[1].start()
        return jnp.sqrt(jnp.sum(total, keepdims=True))

    def use(i, rows, root):
        if i == 0:
            store_split(left_use, rows, root)
        else:
            right_use[rows, :] = root.astype(BF16)

    def finish(i):
        if i == 0:
            stores[2].start()

    def send(grad_norm):
        grad = grad_ref[...]
        half_way = jnp.dot(left_use[0], grad, preferred_element_type=F32) + jnp.dot(
            left_use[1], grad, preferred_element_type=F32
        )
        half_way = half_way.astype(BF16)
        total = jnp.zeros((8, 256), F32)
        for which in (half, 1 - half):
            span = pl.ds(pl.multiple_of(which * 256, 256), 256)
            raw = jnp.dot(half_way, right_use[:, span], preferred_element_type=F32)
            total = total + jnp.sum((raw * raw).reshape(BLK // 8, 8, 256), axis=0)
            if which is half:
                left_p[:, 0:256] = raw
        graft = grad_norm / jnp.sqrt(jnp.sum(total, keepdims=True) + 1e-06)
        for q in range(2):
            rows_ref[pl.ds(q, BLK, stride=2), :] = left_p[:, q * 128 : (q + 1) * 128] * graft
        out_ref[...] = rows_ref[...].astype(BF16)

    refreshed = flag_ref[0, 0] > 0.5

    @pl.when(refreshed)
    def _():
        grad_norm = factors()
        sides = (
            (left_f, left_x, left_y, left_z, left_p, left_r),
            (right_f, right_x, right_y, right_z, right_p, right_r),
        )
        energy = newton(sides, store_high, product_high, use, finish)
        send(grad_norm)

        @pl.when(jnp.logical_not(energy[0, 0] <= ONE_PASS_ENERGY))
        def _():
            stores[2].wait()
            newton(sides, store_split, product, use, finish)
            send(grad_norm)

    @pl.when(jnp.logical_not(refreshed))
    def _():
        loads = [
            pltpu.make_async_copy(left_root_prev, left_r, in_sems.at[0]),
            pltpu.make_async_copy(right_root_prev, right_r, in_sems.at[1]),
        ]
        for load in loads:
            load.start()
        grad_norm = factors()
        for i, (load, ref) in enumerate(zip(loads, (left_r, right_r))):
            load.wait()
            finish(i)
            for start in range(0, BLK, CHUNK):
                rows = slice(start, start + CHUNK)
                use(i, rows, ref[rows, :])
        send(grad_norm)

    for store in stores:
        store.wait()


def vmem():
    return pl.BlockSpec(memory_space=pltpu.VMEM)


def hbm():
    return pl.BlockSpec(memory_space=pltpu.HBM)


def stay(value):
    return pltpu.with_memory_space_constraint(value, pltpu.HBM)


def params(limit=VMEM_LIMIT):
    return pltpu.CompilerParams(vmem_limit_bytes=limit)


def swap(value):
    return lax.ppermute(value, "dp", [(0, 1), (1, 0)])


def exchange(messages):
    moved = lax.all_to_all(messages.reshape(NB, ROWS, 128), "fsdp", split_axis=0, concat_axis=0, tiled=True)
    return moved.reshape(NB * ROWS, 128)


def local(grad_parts, held_block, refresh, left_prev, right_prev, left_root_prev, right_root_prev):
    mine = grad_parts[0]
    held_row = held_block.reshape(1, NB)
    message = jax.ShapeDtypeStruct((NB * ROWS, 128), BF16)
    matrix = jax.ShapeDtypeStruct((BLK, BLK), F32)

    theirs = swap(mine)
    own, placed = pl.pallas_call(
        own_order_kernel,
        out_shape=(jax.ShapeDtypeStruct((NB * ROWS, 128), F32), jax.ShapeDtypeStruct((NB, NB), BF16)),
        in_specs=[vmem(), hbm()],
        out_specs=(vmem(), vmem()),
        scratch_shapes=[pltpu.VMEM((NB, 2048), BF16), pltpu.SemaphoreType.DMA],
        compiler_params=params(),
        cost_estimate=pl.CostEstimate(flops=NB * NB * ROWS * 256, bytes_accessed=8 * NB * ROWS * 128, transcendentals=0),
        name="own_order",
    )(held_row, stay(mine))
    ordered = pl.pallas_call(
        send_order_kernel,
        out_shape=message,
        in_specs=[vmem()] * 3,
        out_specs=vmem(),
        scratch_shapes=[pltpu.VMEM((NB * ROWS, 128), F32)],
        compiler_params=params(),
        name="send_order",
    )(placed, own, theirs)
    got = exchange(ordered)

    theirs = swap(got)
    own, own_total, left_start, flag = pl.pallas_call(
        own_unpack_kernel,
        out_shape=(
            jax.ShapeDtypeStruct((BLK, 256), BF16),
            jax.ShapeDtypeStruct((8, 128), F32),
            matrix,
            jax.ShapeDtypeStruct((8, 128), F32),
        ),
        in_specs=[vmem()] * 2 + [hbm()] * 2,
        out_specs=(vmem(),) * 4,
        scratch_shapes=[
            pltpu.VMEM((NB * ROWS, 128), F32),
            pltpu.SMEM((NB,), jnp.int32),
            pltpu.SMEM(refresh.shape, jnp.int32),
            pltpu.SemaphoreType.DMA((2,)),
        ],
        compiler_params=params(),
        cost_estimate=pl.CostEstimate(flops=BLK * BLK * 512, bytes_accessed=8 * BLK * BLK, transcendentals=0),
        name="own_unpack",
    )(got, left_prev[0], stay(held_block), stay(refresh))
    outgoing, left_new, right_new, left_use, right_root = pl.pallas_call(
        owner_kernel,
        out_shape=(message, matrix, matrix, matrix, matrix),
        in_specs=[vmem()] * 6 + [hbm()] * 2,
        out_specs=(vmem(),) + (hbm(),) * 3 + (vmem(),),
        scratch_shapes=[pltpu.VMEM((NB * ROWS, 128), F32), pltpu.VMEM((BLK, BLK), BF16)]
        + 3 * [pltpu.VMEM((BLK, BLK), F32)]
        + 2 * (3 * [pltpu.VMEM((2, BLK, BLK), BF16)] + [pltpu.VMEM((BLK, BLK), F32)])
        + [
            pltpu.VMEM((2, BLK, BLK), BF16),
            pltpu.VMEM((BLK, BLK), BF16),
            pltpu.SemaphoreType.DMA((2,)),
            pltpu.SemaphoreType.DMA((3,)),
        ],
        compiler_params=params(),
        name="owner",
    )(own, own_total, theirs, left_start, right_prev[0], flag, stay(left_root_prev[0]), stay(right_root_prev[0]))

    back = exchange(outgoing)
    theirs = swap(back)
    restored = jax.ShapeDtypeStruct((NB, 2048), BF16)
    restore_scratch = [
        pltpu.VMEM((NB * ROWS, 128), F32),
        pltpu.VMEM((NB, ROWS * 128), BF16),
        pltpu.SemaphoreType.DMA((4,)),
    ]
    halfway, right_use = pl.pallas_call(
        own_restore_kernel,
        out_shape=(restored, matrix),
        in_specs=[vmem()] * 3,
        out_specs=(hbm(), hbm()),
        scratch_shapes=restore_scratch + [pltpu.SemaphoreType.DMA],
        compiler_params=params(),
        cost_estimate=pl.CostEstimate(flops=NB * NB * ROWS * 256, bytes_accessed=4 * NB * ROWS * 128, transcendentals=0),
        name="own_restore",
    )(placed, back, right_root)
    update = pl.pallas_call(
        restore_kernel,
        out_shape=restored,
        in_specs=[vmem()] * 2 + [hbm()],
        out_specs=hbm(),
        scratch_shapes=restore_scratch,
        compiler_params=params(),
        input_output_aliases={2: 0},
        name="restore",
    )(placed, theirs, halfway)
    return (update, left_new[None], right_new[None], left_use[None], right_use[None])


def solution(mesh):
    placed = (
        P("dp", None, "fsdp"),
        P(),
        P(),
        P("fsdp", None, None),
        P("fsdp", None, None),
        P("fsdp", None, None),
        P("fsdp", None, None),
    )
    return jax.shard_map(
        local,
        mesh=mesh,
        in_specs=placed,
        out_specs=(
            P(None, "fsdp"),
            P("fsdp", None, None),
            P("fsdp", None, None),
            P("fsdp", None, None),
            P("fsdp", None, None),
        ),
        check_vma=False,
    )
```

```python
import functools

import jax
import jax.numpy as jnp
from jax import lax
from jax.experimental import pallas as pl
from jax.experimental.pallas import tpu as pltpu
from jax.sharding import PartitionSpec as P

BLK = 512
NB = 128
ROWS = 8
EPS = 0.001
F32 = jnp.float32
BF16 = jnp.bfloat16
VMEM_LIMIT = 24 * 1024 * 1024


def one_hot(held):
    block = lax.broadcasted_iota(jnp.int32, (NB, NB), 0)
    return jnp.where(block == held, 1.0, 0.0).astype(BF16)


def to_slots(placed, value):
    return lax.dot_general(placed, value, (((0,), (0,)), ((), ())), preferred_element_type=F32)


def segment_column(part, half):
    return pl.multiple_of((part // 2) * BLK + half * 256 + (part % 2) * 128, 128)


def own_order_kernel(held_ref, mine_hbm, rows_ref, placed_ref, mine_ref, sem):
    half = lax.axis_index("dp")
    load = pltpu.make_async_copy(mine_hbm, mine_ref, sem)
    load.start()
    placed = one_hot(held_ref[...])
    placed_ref[...] = placed
    load.wait()
    for part in range(ROWS):
        columns = pl.ds(segment_column(part, half), 128)
        rows_ref[pl.ds(part, NB, stride=ROWS), :] = to_slots(placed, mine_ref[:, columns])


def send_order_kernel(placed_ref, own_ref, theirs_ref, out_ref, rows_ref):
    half = lax.axis_index("dp")
    placed = placed_ref[...]
    for part in range(ROWS):
        columns = pl.ds(segment_column(part, half), 128)
        rows_ref[pl.ds(part, NB, stride=ROWS), :] = to_slots(placed, theirs_ref[:, columns])
    out_ref[...] = (rows_ref[...] + own_ref[...]).astype(BF16)


def unpack_half(message_ref, rows_ref, write):
    rows_ref[...] = message_ref[...].astype(F32)
    total = jnp.zeros((8, 128), F32)
    for q in range(2):
        part = rows_ref[pl.ds(q, BLK, stride=2), :]
        write(q, part.astype(BF16))
        total = total + jnp.sum((part * part).reshape(BLK // 8, 8, 128), axis=0)
    return total


def diagonal(matrix_ref):
    total = jnp.zeros((8, 128), F32)
    for start in range(0, BLK, 128):
        block = matrix_ref[start : start + 128, start : start + 128]
        row = lax.broadcasted_iota(jnp.int32, (128, 128), 0)
        column = lax.broadcasted_iota(jnp.int32, (128, 128), 1)
        total = total + jnp.sum(jnp.where(row == column, block, 0.0).reshape(16, 8, 128), axis=0)
    return total


def own_unpack_kernel(
    mine_ref, left_prev, right_prev, held_hbm, refresh_hbm,
    grad_ref, total_ref, left_ref, traces_ref, flag_ref, rows_ref, held_ref, refresh_ref, sems,
):
    loads = [
        pltpu.make_async_copy(held_hbm, held_ref, sems.at[0]),
        pltpu.make_async_copy(refresh_hbm, refresh_ref, sems.at[1]),
    ]
    for load in loads:
        load.start()

    def write(q, part):
        grad_ref[:, q * 128 : (q + 1) * 128] = part

    total_ref[...] = unpack_half(mine_ref, rows_ref, write)
    left_ref[...] = left_prev[...] + outer(grad_ref[...])
    traces_ref[0] = diagonal(left_prev)
    traces_ref[1] = diagonal(right_prev)
    for load in loads:
        load.wait()
    held = held_ref[lax.axis_index("fsdp")]
    refreshed = refresh_ref[0] == held
    for i in range(1, refresh_ref.shape[0]):
        refreshed = refreshed | (refresh_ref[i] == held)
    flag_ref[...] = jnp.full(flag_ref.shape, jnp.where(refreshed, 1.0, 0.0), F32)


def outer(value):
    return lax.dot_general(value, value, (((1,), (1,)), ((), ())), preferred_element_type=F32)


def inner(value):
    return lax.dot_general(value, value, (((0,), (0,)), ((), ())), preferred_element_type=F32)


def restore_half(placed_ref, message_ref, out_hbm, half, rows_ref, whole_ref, sems):
    placed = placed_ref[...]
    rows_ref[...] = message_ref[...].astype(F32)
    copies = []
    for row in range(4):
        for part in (2 * row, 2 * row + 1):
            piece = rows_ref[pl.ds(part, NB, stride=ROWS), :].astype(BF16)
            whole_ref[:, part * 128 : (part + 1) * 128] = jnp.dot(
                placed, piece, preferred_element_type=F32
            ).astype(BF16)
        columns = pl.ds(segment_column(2 * row, half), 256)
        source = whole_ref.at[:, row * 256 : (row + 1) * 256]
        copies.append(pltpu.make_async_copy(source, out_hbm.at[:, columns], sems.at[row]))
        copies[row].start()
    for copy in copies:
        copy.wait()


def own_restore_kernel(placed_ref, mine_ref, root_ref, out_hbm, root_hbm, rows_ref, whole_ref, sems, root_sem):
    store = pltpu.make_async_copy(root_ref, root_hbm, root_sem)
    store.start()
    restore_half(placed_ref, mine_ref, out_hbm, lax.axis_index("dp"), rows_ref, whole_ref, sems)
    store.wait()


def restore_kernel(placed_ref, theirs_ref, half_hbm, out_hbm, rows_ref, whole_ref, sems):
    del half_hbm
    restore_half(placed_ref, theirs_ref, out_hbm, 1 - lax.axis_index("dp"), rows_ref, whole_ref, sems)


def split(value):
    high = value.astype(BF16)
    return high, (value - high.astype(F32)).astype(BF16)


def store_split(ref, rows, value):
    ref[0, rows, :], ref[1, rows, :] = split(value)


def store_high(ref, rows, value):
    ref[0, rows, :] = value.astype(BF16)


def product(left_ref, right_ref):
    return (
        product_high(left_ref, right_ref)
        + jnp.dot(left_ref[0], right_ref[1], preferred_element_type=F32)
        + jnp.dot(left_ref[1], right_ref[0], preferred_element_type=F32)
    )


def product_high(left_ref, right_ref):
    return jnp.dot(left_ref[0], right_ref[0], preferred_element_type=F32)


CHUNK = 64


def add_diagonal(start, value, amount):
    block = start // 128 * 128
    row = lax.broadcasted_iota(jnp.int32, (CHUNK, 128), 0) + (start - block)
    column = lax.broadcasted_iota(jnp.int32, (CHUNK, 128), 1)
    touched = value[:, block : block + 128] + jnp.where(row == column, amount, 0.0)
    parts = [value[:, :block], touched, value[:, block + 128 :]]
    return jnp.concatenate([part for part in parts if part.shape[1]], axis=1)


ONE_PASS_ENERGY = 256.0


def newton(sides, traces, store, product, use, finish):
    scales, inverses, energies = [], [], []

    def shifted(i, start):
        return add_diagonal(start, sides[i][0][start : start + CHUNK, :] * inverses[i], EPS * inverses[i] - 1.0)

    def shift(i, factor_ref, x_ref, y_ref, z_ref, part_ref, root_ref):
        scale = (traces[i] + BLK * EPS) * (1.0 / BLK)
        inverses.append(1.0 / scale)
        scales.append(lax.rsqrt(jnp.sqrt(scale)))
        for start in range(0, BLK, CHUNK):
            store(x_ref, slice(start, start + CHUNK), shifted(i, start))

    def square(i, factor_ref, x_ref, y_ref, z_ref, part_ref, root_ref):
        value = product(x_ref, x_ref)
        energy = jnp.zeros((8, BLK), F32)
        for start in range(0, BLK, CHUNK):
            rows = slice(start, start + CHUNK)
            first, second = shifted(i, start), value[rows, :]
            energy = energy + jnp.sum((second * second).reshape(CHUNK // 8, 8, BLK), axis=0)
            part = first - second * 0.125
            part_ref[rows, :] = part
            store(y_ref, rows, part * -0.5)
            store(z_ref, rows, first * 0.75 - second * 0.25)
        energies.append(jnp.sum(energy, keepdims=True))

    def quartic(i, factor_ref, x_ref, y_ref, z_ref, part_ref, root_ref):
        value = product(y_ref, y_ref)
        for start in range(0, BLK, CHUNK):
            rows = slice(start, start + CHUNK)
            part, fourth = part_ref[rows, :], value[rows, :]
            part_ref[rows, :] = part + fourth
            store(x_ref, rows, fourth - part)

    def last(i, factor_ref, x_ref, y_ref, z_ref, part_ref, root_ref):
        value = product(x_ref, z_ref)
        for start in range(0, BLK, CHUNK):
            rows = slice(start, start + CHUNK)
            beside = (part_ref[rows, :] + value[rows, :]) * (scales[i] * -0.25)
            root = add_diagonal(start, beside, scales[i])
            root_ref[rows, :] = root
            use(i, rows, root, beside)
        finish(i)

    for step in (shift, square, quartic, last):
        for i, side in enumerate(sides):
            step(i, *side)
    return jnp.maximum(*energies), scales[0]


def owner_kernel(
    own_ref, own_total_ref, theirs_ref, left_start, right_prev, traces_ref, flag_ref, left_root_prev, right_root_prev,
    out_ref, left_out, right_out, left_root_out, right_r,
    rows_ref, grad_ref, left_f, right_f, left_r,
    left_x, left_y, left_z, left_p, right_x, right_y, right_z, right_p, left_use, right_use, in_sems, out_sems,
):
    half = lax.axis_index("dp")
    stores = [
        pltpu.make_async_copy(source, target, out_sems.at[i])
        for i, (source, target) in enumerate(
            ((left_f, left_out), (right_f, right_out), (left_r, left_root_out))
        )
    ]

    def columns(which, q):
        return pl.ds(pl.multiple_of(which * 256 + q * 128, 128), 128)

    def factors():
        parts = []

        def write(q, part):
            grad_ref[:, columns(1 - half, q)] = part
            parts.append(part)

        energy = jnp.sum(own_total_ref[...] + unpack_half(theirs_ref, rows_ref, write), keepdims=True)
        for q in range(2):
            grad_ref[:, columns(half, q)] = own_ref[:, q * 128 : (q + 1) * 128]
        left_f[...] = left_start[...] + outer(jnp.concatenate(parts, axis=1))
        stores[0].start()
        right_f[...] = right_prev[...] + inner(grad_ref[...])
        stores[1].start()
        return energy

    def use(i, rows, root, beside):
        if i == 0:
            left_use[0, rows, :] = beside.astype(BF16)
        else:
            right_use[rows, :] = root.astype(BF16)

    def finish(i):
        if i == 0:
            stores[2].start()

    def send(grad_energy, left_scale):
        grad = grad_ref[...]
        half_way = jnp.dot(left_use[0], grad, preferred_element_type=F32)
        if left_scale is None:
            half_way = half_way + jnp.dot(left_use[1], grad, preferred_element_type=F32)
        else:
            half_way = half_way + left_scale * grad.astype(F32)
        half_way = half_way.astype(BF16)
        total = jnp.zeros((8, 256), F32)
        for which in (half, 1 - half):
            span = pl.ds(pl.multiple_of(which * 256, 256), 256)
            raw = jnp.dot(half_way, right_use[:, span], preferred_element_type=F32)
            total = total + jnp.sum((raw * raw).reshape(BLK // 8, 8, 256), axis=0)
            if which is half:
                left_p[:, 0:256] = raw
        graft = jnp.sqrt(grad_energy) / jnp.sqrt(jnp.sum(total, keepdims=True) + 1e-06)
        for q in range(2):
            rows_ref[pl.ds(q, BLK, stride=2), :] = left_p[:, q * 128 : (q + 1) * 128] * graft
        out_ref[...] = rows_ref[...].astype(BF16)

    refreshed = flag_ref[0, 0] > 0.5

    @pl.when(refreshed)
    def _():
        grad_energy = factors()
        traces = [jnp.sum(traces_ref[i], keepdims=True) + grad_energy for i in range(2)]
        sides = (
            (left_f, left_x, left_y, left_z, left_p, left_r),
            (right_f, right_x, right_y, right_z, right_p, right_r),
        )
        energy, left_scale = newton(sides, traces, store_high, product_high, use, finish)
        send(grad_energy, left_scale)

        @pl.when(jnp.logical_not(energy[0, 0] <= ONE_PASS_ENERGY))
        def _():
            stores[2].wait()
            _, left_scale = newton(sides, traces, store_split, product, use, finish)
            send(grad_energy, left_scale)

    @pl.when(jnp.logical_not(refreshed))
    def _():
        loads = [
            pltpu.make_async_copy(left_root_prev, left_r, in_sems.at[0]),
            pltpu.make_async_copy(right_root_prev, right_r, in_sems.at[1]),
        ]
        for load in loads:
            load.start()
        pltpu.make_async_copy(left_root_prev, left_root_out, out_sems.at[2]).start()
        grad_energy = factors()
        loads[0].wait()
        for start in range(0, BLK, CHUNK):
            rows = slice(start, start + CHUNK)
            store_split(left_use, rows, left_r[rows, :])
        loads[1].wait()
        for start in range(0, BLK, CHUNK):
            rows = slice(start, start + CHUNK)
            right_use[rows, :] = right_r[rows, :].astype(BF16)
        send(grad_energy, None)

    for store in stores:
        store.wait()


def vmem():
    return pl.BlockSpec(memory_space=pltpu.VMEM)


def hbm():
    return pl.BlockSpec(memory_space=pltpu.HBM)


def stay(value):
    return pltpu.with_memory_space_constraint(value, pltpu.HBM)


def params(limit=VMEM_LIMIT):
    return pltpu.CompilerParams(vmem_limit_bytes=limit)


def swap(value):
    return lax.ppermute(value, "dp", [(0, 1), (1, 0)])


def exchange(messages):
    moved = lax.all_to_all(messages.reshape(NB, ROWS, 128), "fsdp", split_axis=0, concat_axis=0, tiled=True)
    return moved.reshape(NB * ROWS, 128)


def local(grad_parts, held_block, refresh, left_prev, right_prev, left_root_prev, right_root_prev):
    mine = grad_parts[0]
    held_row = held_block.reshape(1, NB)
    message = jax.ShapeDtypeStruct((NB * ROWS, 128), BF16)
    matrix = jax.ShapeDtypeStruct((BLK, BLK), F32)

    theirs = swap(mine)
    own, placed = pl.pallas_call(
        own_order_kernel,
        out_shape=(jax.ShapeDtypeStruct((NB * ROWS, 128), F32), jax.ShapeDtypeStruct((NB, NB), BF16)),
        in_specs=[vmem(), hbm()],
        out_specs=(vmem(), vmem()),
        scratch_shapes=[pltpu.VMEM((NB, 2048), BF16), pltpu.SemaphoreType.DMA],
        compiler_params=params(),
        cost_estimate=pl.CostEstimate(flops=NB * NB * ROWS * 256, bytes_accessed=8 * NB * ROWS * 128, transcendentals=0),
        name="own_order",
    )(held_row, stay(mine))
    ordered = pl.pallas_call(
        send_order_kernel,
        out_shape=message,
        in_specs=[vmem()] * 3,
        out_specs=vmem(),
        scratch_shapes=[pltpu.VMEM((NB * ROWS, 128), F32)],
        compiler_params=params(),
        name="send_order",
    )(placed, own, theirs)
    got = exchange(ordered)

    theirs = swap(got)
    own, own_total, left_start, traces, flag = pl.pallas_call(
        own_unpack_kernel,
        out_shape=(
            jax.ShapeDtypeStruct((BLK, 256), BF16),
            jax.ShapeDtypeStruct((8, 128), F32),
            matrix,
            jax.ShapeDtypeStruct((2, 8, 128), F32),
            jax.ShapeDtypeStruct((8, 128), F32),
        ),
        in_specs=[vmem()] * 3 + [hbm()] * 2,
        out_specs=(vmem(),) * 5,
        scratch_shapes=[
            pltpu.VMEM((NB * ROWS, 128), F32),
            pltpu.SMEM((NB,), jnp.int32),
            pltpu.SMEM(refresh.shape, jnp.int32),
            pltpu.SemaphoreType.DMA((2,)),
        ],
        compiler_params=params(),
        cost_estimate=pl.CostEstimate(flops=BLK * BLK * 512, bytes_accessed=8 * BLK * BLK, transcendentals=0),
        name="own_unpack",
    )(got, left_prev[0], right_prev[0], stay(held_block), stay(refresh))
    outgoing, left_new, right_new, left_use, right_root = pl.pallas_call(
        owner_kernel,
        out_shape=(message, matrix, matrix, matrix, matrix),
        in_specs=[vmem()] * 7 + [hbm()] * 2,
        out_specs=(vmem(),) + (hbm(),) * 3 + (vmem(),),
        scratch_shapes=[pltpu.VMEM((NB * ROWS, 128), F32), pltpu.VMEM((BLK, BLK), BF16)]
        + 3 * [pltpu.VMEM((BLK, BLK), F32)]
        + 2 * (3 * [pltpu.VMEM((2, BLK, BLK), BF16)] + [pltpu.VMEM((BLK, BLK), F32)])
        + [
            pltpu.VMEM((2, BLK, BLK), BF16),
            pltpu.VMEM((BLK, BLK), BF16),
            pltpu.SemaphoreType.DMA((2,)),
            pltpu.SemaphoreType.DMA((3,)),
        ],
        compiler_params=params(),
        name="owner",
    )(
        own,
        own_total,
        theirs,
        left_start,
        right_prev[0],
        traces,
        flag,
        stay(left_root_prev[0]),
        stay(right_root_prev[0]),
    )

    back = exchange(outgoing)
    theirs = swap(back)
    restored = jax.ShapeDtypeStruct((NB, 2048), BF16)
    restore_scratch = [
        pltpu.VMEM((NB * ROWS, 128), F32),
        pltpu.VMEM((NB, ROWS * 128), BF16),
        pltpu.SemaphoreType.DMA((4,)),
    ]
    halfway, right_use = pl.pallas_call(
        own_restore_kernel,
        out_shape=(restored, matrix),
        in_specs=[vmem()] * 3,
        out_specs=(hbm(), hbm()),
        scratch_shapes=restore_scratch + [pltpu.SemaphoreType.DMA],
        compiler_params=params(),
        cost_estimate=pl.CostEstimate(flops=NB * NB * ROWS * 256, bytes_accessed=4 * NB * ROWS * 128, transcendentals=0),
        name="own_restore",
    )(placed, back, right_root)
    update = pl.pallas_call(
        restore_kernel,
        out_shape=restored,
        in_specs=[vmem()] * 2 + [hbm()],
        out_specs=hbm(),
        scratch_shapes=restore_scratch,
        compiler_params=params(),
        input_output_aliases={2: 0},
        name="restore",
    )(placed, theirs, halfway)
    return (update, left_new[None], right_new[None], left_use[None], right_use[None])


def solution(mesh):
    placed = (
        P("dp", None, "fsdp"),
        P(),
        P(),
        P("fsdp", None, None),
        P("fsdp", None, None),
        P("fsdp", None, None),
        P("fsdp", None, None),
    )
    return jax.shard_map(
        local,
        mesh=mesh,
        in_specs=placed,
        out_specs=(
            P(None, "fsdp"),
            P("fsdp", None, None),
            P("fsdp", None, None),
            P("fsdp", None, None),
            P("fsdp", None, None),
        ),
        check_vma=False,
    )
```

```python
import functools

import jax
import jax.numpy as jnp
from jax import lax
from jax.experimental import pallas as pl
from jax.experimental.pallas import tpu as pltpu
from jax.sharding import PartitionSpec as P

BLK = 512
NB = 128
ROWS = 8
EPS = 0.001
F32 = jnp.float32
BF16 = jnp.bfloat16
VMEM_LIMIT = 24 * 1024 * 1024


def one_hot(held):
    block = lax.broadcasted_iota(jnp.int32, (NB, NB), 0)
    return jnp.where(block == held, 1.0, 0.0).astype(BF16)


def to_slots(placed, value):
    return lax.dot_general(placed, value, (((0,), (0,)), ((), ())), preferred_element_type=F32)


def segment_column(part, half):
    return pl.multiple_of((part // 2) * BLK + half * 256 + (part % 2) * 128, 128)


def own_order_kernel(held_ref, mine_hbm, rows_ref, placed_ref, mine_ref, sem):
    half = lax.axis_index("dp")
    load = pltpu.make_async_copy(mine_hbm, mine_ref, sem)
    load.start()
    placed = one_hot(held_ref[...])
    placed_ref[...] = placed
    load.wait()
    for part in range(ROWS):
        columns = pl.ds(segment_column(part, half), 128)
        rows_ref[pl.ds(part, NB, stride=ROWS), :] = to_slots(placed, mine_ref[:, columns])


def send_order_kernel(placed_ref, own_ref, theirs_ref, out_ref, rows_ref):
    half = lax.axis_index("dp")
    placed = placed_ref[...]
    for part in range(ROWS):
        columns = pl.ds(segment_column(part, half), 128)
        rows_ref[pl.ds(part, NB, stride=ROWS), :] = to_slots(placed, theirs_ref[:, columns])
    out_ref[...] = (rows_ref[...] + own_ref[...]).astype(BF16)


def unpack_half(message_ref, rows_ref, write):
    rows_ref[...] = message_ref[...].astype(F32)
    total = jnp.zeros((8, 128), F32)
    for q in range(2):
        part = rows_ref[pl.ds(q, BLK, stride=2), :]
        write(q, part.astype(BF16))
        total = total + jnp.sum((part * part).reshape(BLK // 8, 8, 128), axis=0)
    return total


def diagonal(matrix_ref):
    total = jnp.zeros((8, 128), F32)
    for start in range(0, BLK, 128):
        block = matrix_ref[start : start + 128, start : start + 128]
        row = lax.broadcasted_iota(jnp.int32, (128, 128), 0)
        column = lax.broadcasted_iota(jnp.int32, (128, 128), 1)
        total = total + jnp.sum(jnp.where(row == column, block, 0.0).reshape(16, 8, 128), axis=0)
    return total


def own_unpack_kernel(
    mine_ref, left_prev, right_prev, left_root_hbm, held_hbm, refresh_hbm,
    grad_ref, total_ref, left_ref, traces_ref, flag_ref, kept_ref, rows_ref, held_ref, refresh_ref, sems,
):
    kept = pltpu.make_async_copy(left_root_hbm, kept_ref, sems.at[2])
    kept.start()
    loads = [
        pltpu.make_async_copy(held_hbm, held_ref, sems.at[0]),
        pltpu.make_async_copy(refresh_hbm, refresh_ref, sems.at[1]),
    ]
    for load in loads:
        load.start()

    def write(q, part):
        grad_ref[:, q * 128 : (q + 1) * 128] = part

    total_ref[...] = unpack_half(mine_ref, rows_ref, write)
    left_ref[...] = left_prev[...] + outer(grad_ref[...])
    traces_ref[0] = diagonal(left_prev)
    traces_ref[1] = diagonal(right_prev)
    for load in loads:
        load.wait()
    held = held_ref[lax.axis_index("fsdp")]
    refreshed = refresh_ref[0] == held
    for i in range(1, refresh_ref.shape[0]):
        refreshed = refreshed | (refresh_ref[i] == held)
    flag_ref[...] = jnp.full(flag_ref.shape, jnp.where(refreshed, 1.0, 0.0), F32)
    kept.wait()


def outer(value):
    return lax.dot_general(value, value, (((1,), (1,)), ((), ())), preferred_element_type=F32)


def inner(value):
    return lax.dot_general(value, value, (((0,), (0,)), ((), ())), preferred_element_type=F32)


def restore_half(placed_ref, message_ref, out_hbm, half, rows_ref, whole_ref, sems):
    placed = placed_ref[...]
    rows_ref[...] = message_ref[...].astype(F32)
    copies = []
    for row in range(4):
        for part in (2 * row, 2 * row + 1):
            piece = rows_ref[pl.ds(part, NB, stride=ROWS), :].astype(BF16)
            whole_ref[:, part * 128 : (part + 1) * 128] = jnp.dot(
                placed, piece, preferred_element_type=F32
            ).astype(BF16)
        columns = pl.ds(segment_column(2 * row, half), 256)
        source = whole_ref.at[:, row * 256 : (row + 1) * 256]
        copies.append(pltpu.make_async_copy(source, out_hbm.at[:, columns], sems.at[row]))
        copies[row].start()
    for copy in copies:
        copy.wait()


def own_restore_kernel(placed_ref, mine_ref, root_ref, out_hbm, root_hbm, rows_ref, whole_ref, sems, root_sem):
    store = pltpu.make_async_copy(root_ref, root_hbm, root_sem)
    store.start()
    restore_half(placed_ref, mine_ref, out_hbm, lax.axis_index("dp"), rows_ref, whole_ref, sems)
    store.wait()


def restore_kernel(placed_ref, theirs_ref, half_hbm, out_hbm, rows_ref, whole_ref, sems):
    del half_hbm
    restore_half(placed_ref, theirs_ref, out_hbm, 1 - lax.axis_index("dp"), rows_ref, whole_ref, sems)


def split(value):
    high = value.astype(BF16)
    return high, (value - high.astype(F32)).astype(BF16)


def store_split(ref, rows, value):
    ref[0, rows, :], ref[1, rows, :] = split(value)


def store_high(ref, rows, value):
    ref[0, rows, :] = value.astype(BF16)


def product(left_ref, right_ref):
    return (
        product_high(left_ref, right_ref)
        + jnp.dot(left_ref[0], right_ref[1], preferred_element_type=F32)
        + jnp.dot(left_ref[1], right_ref[0], preferred_element_type=F32)
    )


def product_high(left_ref, right_ref):
    return jnp.dot(left_ref[0], right_ref[0], preferred_element_type=F32)


CHUNK = 64


def add_diagonal(start, value, amount):
    block = start // 128 * 128
    row = lax.broadcasted_iota(jnp.int32, (CHUNK, 128), 0) + (start - block)
    column = lax.broadcasted_iota(jnp.int32, (CHUNK, 128), 1)
    touched = value[:, block : block + 128] + jnp.where(row == column, amount, 0.0)
    parts = [value[:, :block], touched, value[:, block + 128 :]]
    return jnp.concatenate([part for part in parts if part.shape[1]], axis=1)


ONE_PASS_ENERGY = 256.0


def newton(sides, traces, store, product, use, finish):
    scales, inverses, energies = [], [], []

    def shifted(i, start):
        return add_diagonal(start, sides[i][0][start : start + CHUNK, :] * inverses[i], EPS * inverses[i] - 1.0)

    def shift(i, factor_ref, x_ref, y_ref, z_ref, part_ref, root_ref):
        scale = (traces[i] + BLK * EPS) * (1.0 / BLK)
        inverses.append(1.0 / scale)
        scales.append(lax.rsqrt(jnp.sqrt(scale)))
        for start in range(0, BLK, CHUNK):
            store(x_ref, slice(start, start + CHUNK), shifted(i, start))

    def square(i, factor_ref, x_ref, y_ref, z_ref, part_ref, root_ref):
        value = product(x_ref, x_ref)
        energy = jnp.zeros((8, BLK), F32)
        for start in range(0, BLK, CHUNK):
            rows = slice(start, start + CHUNK)
            first, second = shifted(i, start), value[rows, :]
            energy = energy + jnp.sum((second * second).reshape(CHUNK // 8, 8, BLK), axis=0)
            part = first - second * 0.125
            part_ref[rows, :] = part
            store(y_ref, rows, part * -0.5)
            store(z_ref, rows, first * 0.75 - second * 0.25)
        energies.append(jnp.sum(energy, keepdims=True))

    def quartic(i, factor_ref, x_ref, y_ref, z_ref, part_ref, root_ref):
        value = product(y_ref, y_ref)
        for start in range(0, BLK, CHUNK):
            rows = slice(start, start + CHUNK)
            part, fourth = part_ref[rows, :], value[rows, :]
            part_ref[rows, :] = part + fourth
            store(x_ref, rows, fourth - part)

    def last(i, factor_ref, x_ref, y_ref, z_ref, part_ref, root_ref):
        value = product(x_ref, z_ref)
        for start in range(0, BLK, CHUNK):
            rows = slice(start, start + CHUNK)
            beside = (part_ref[rows, :] + value[rows, :]) * (scales[i] * -0.25)
            root = add_diagonal(start, beside, scales[i])
            root_ref[rows, :] = root
            use(i, rows, root, beside)
        finish(i)

    for step in (shift, square, quartic, last):
        for i, side in enumerate(sides):
            step(i, *side)
    return jnp.maximum(*energies), scales[0]


def owner_kernel(
    own_ref, own_total_ref, theirs_ref, left_start, right_prev, traces_ref, flag_ref, left_kept, right_root_prev,
    out_ref, left_out, right_out, left_root_out, right_r,
    rows_ref, grad_ref, left_f, right_f, left_r,
    left_x, left_y, left_z, left_p, right_x, right_y, right_z, right_p, left_use, right_use, in_sem, out_sems,
):
    half = lax.axis_index("dp")
    stores = [
        pltpu.make_async_copy(source, target, out_sems.at[i])
        for i, (source, target) in enumerate(
            ((left_f, left_out), (right_f, right_out), (left_r, left_root_out))
        )
    ]

    def columns(which, q):
        return pl.ds(pl.multiple_of(which * 256 + q * 128, 128), 128)

    def factors():
        parts = []

        def write(q, part):
            grad_ref[:, columns(1 - half, q)] = part
            parts.append(part)

        energy = jnp.sum(own_total_ref[...] + unpack_half(theirs_ref, rows_ref, write), keepdims=True)
        for q in range(2):
            grad_ref[:, columns(half, q)] = own_ref[:, q * 128 : (q + 1) * 128]
        left_f[...] = left_start[...] + outer(jnp.concatenate(parts, axis=1))
        stores[0].start()
        right_f[...] = right_prev[...] + inner(grad_ref[...])
        stores[1].start()
        return energy

    def use(i, rows, root, beside):
        if i == 0:
            left_use[0, rows, :] = beside.astype(BF16)
        else:
            right_use[rows, :] = root.astype(BF16)

    def finish(i):
        if i == 0:
            stores[2].start()

    def send(grad_energy, left_scale):
        grad = grad_ref[...]
        half_way = jnp.dot(left_use[0], grad, preferred_element_type=F32)
        if left_scale is None:
            half_way = half_way + jnp.dot(left_use[1], grad, preferred_element_type=F32)
        else:
            half_way = half_way + left_scale * grad.astype(F32)
        half_way = half_way.astype(BF16)
        total = jnp.zeros((8, 256), F32)
        for which in (half, 1 - half):
            span = pl.ds(pl.multiple_of(which * 256, 256), 256)
            raw = jnp.dot(half_way, right_use[:, span], preferred_element_type=F32)
            total = total + jnp.sum((raw * raw).reshape(BLK // 8, 8, 256), axis=0)
            if which is half:
                left_p[:, 0:256] = raw
        graft = jnp.sqrt(grad_energy) / jnp.sqrt(jnp.sum(total, keepdims=True) + 1e-06)
        for q in range(2):
            rows_ref[pl.ds(q, BLK, stride=2), :] = left_p[:, q * 128 : (q + 1) * 128] * graft
        out_ref[...] = rows_ref[...].astype(BF16)

    refreshed = flag_ref[0, 0] > 0.5

    @pl.when(refreshed)
    def _():
        grad_energy = factors()
        traces = [jnp.sum(traces_ref[i], keepdims=True) + grad_energy for i in range(2)]
        sides = (
            (left_f, left_x, left_y, left_z, left_p, left_r),
            (right_f, right_x, right_y, right_z, right_p, right_r),
        )
        energy, left_scale = newton(sides, traces, store_high, product_high, use, finish)
        send(grad_energy, left_scale)

        @pl.when(jnp.logical_not(energy[0, 0] <= ONE_PASS_ENERGY))
        def _():
            stores[2].wait()
            _, left_scale = newton(sides, traces, store_split, product, use, finish)
            send(grad_energy, left_scale)

    @pl.when(jnp.logical_not(refreshed))
    def _():
        load = pltpu.make_async_copy(right_root_prev, right_r, in_sem)
        load.start()
        pltpu.make_async_copy(left_kept, left_root_out, out_sems.at[2]).start()
        grad_energy = factors()
        for start in range(0, BLK, CHUNK):
            rows = slice(start, start + CHUNK)
            store_split(left_use, rows, left_kept[rows, :])
        load.wait()
        for start in range(0, BLK, CHUNK):
            rows = slice(start, start + CHUNK)
            right_use[rows, :] = right_r[rows, :].astype(BF16)
        send(grad_energy, None)

    for store in stores:
        store.wait()


def vmem():
    return pl.BlockSpec(memory_space=pltpu.VMEM)


def hbm():
    return pl.BlockSpec(memory_space=pltpu.HBM)


def stay(value):
    return pltpu.with_memory_space_constraint(value, pltpu.HBM)


def params(limit=VMEM_LIMIT):
    return pltpu.CompilerParams(vmem_limit_bytes=limit)


def swap(value):
    return lax.ppermute(value, "dp", [(0, 1), (1, 0)])


def exchange(messages):
    moved = lax.all_to_all(messages.reshape(NB, ROWS, 128), "fsdp", split_axis=0, concat_axis=0, tiled=True)
    return moved.reshape(NB * ROWS, 128)


def local(grad_parts, held_block, refresh, left_prev, right_prev, left_root_prev, right_root_prev):
    mine = grad_parts[0]
    held_row = held_block.reshape(1, NB)
    message = jax.ShapeDtypeStruct((NB * ROWS, 128), BF16)
    matrix = jax.ShapeDtypeStruct((BLK, BLK), F32)

    theirs = swap(mine)
    own, placed = pl.pallas_call(
        own_order_kernel,
        out_shape=(jax.ShapeDtypeStruct((NB * ROWS, 128), F32), jax.ShapeDtypeStruct((NB, NB), BF16)),
        in_specs=[vmem(), hbm()],
        out_specs=(vmem(), vmem()),
        scratch_shapes=[pltpu.VMEM((NB, 2048), BF16), pltpu.SemaphoreType.DMA],
        compiler_params=params(),
        cost_estimate=pl.CostEstimate(flops=NB * NB * ROWS * 256, bytes_accessed=8 * NB * ROWS * 128, transcendentals=0),
        name="own_order",
    )(held_row, stay(mine))
    ordered = pl.pallas_call(
        send_order_kernel,
        out_shape=message,
        in_specs=[vmem()] * 3,
        out_specs=vmem(),
        scratch_shapes=[pltpu.VMEM((NB * ROWS, 128), F32)],
        compiler_params=params(),
        name="send_order",
    )(placed, own, theirs)
    got = exchange(ordered)

    theirs = swap(got)
    own, own_total, left_start, traces, flag, left_kept = pl.pallas_call(
        own_unpack_kernel,
        out_shape=(
            jax.ShapeDtypeStruct((BLK, 256), BF16),
            jax.ShapeDtypeStruct((8, 128), F32),
            matrix,
            jax.ShapeDtypeStruct((2, 8, 128), F32),
            jax.ShapeDtypeStruct((8, 128), F32),
            matrix,
        ),
        in_specs=[vmem()] * 3 + [hbm()] * 3,
        out_specs=(vmem(),) * 6,
        scratch_shapes=[
            pltpu.VMEM((NB * ROWS, 128), F32),
            pltpu.SMEM((NB,), jnp.int32),
            pltpu.SMEM(refresh.shape, jnp.int32),
            pltpu.SemaphoreType.DMA((3,)),
        ],
        compiler_params=params(),
        cost_estimate=pl.CostEstimate(flops=BLK * BLK * 512, bytes_accessed=8 * BLK * BLK, transcendentals=0),
        name="own_unpack",
    )(got, left_prev[0], right_prev[0], stay(left_root_prev[0]), stay(held_block), stay(refresh))
    outgoing, left_new, right_new, left_use, right_root = pl.pallas_call(
        owner_kernel,
        out_shape=(message, matrix, matrix, matrix, matrix),
        in_specs=[vmem()] * 8 + [hbm()],
        out_specs=(vmem(),) + (hbm(),) * 3 + (vmem(),),
        scratch_shapes=[pltpu.VMEM((NB * ROWS, 128), F32), pltpu.VMEM((BLK, BLK), BF16)]
        + 3 * [pltpu.VMEM((BLK, BLK), F32)]
        + 2 * (3 * [pltpu.VMEM((2, BLK, BLK), BF16)] + [pltpu.VMEM((BLK, BLK), F32)])
        + [
            pltpu.VMEM((2, BLK, BLK), BF16),
            pltpu.VMEM((BLK, BLK), BF16),
            pltpu.SemaphoreType.DMA,
            pltpu.SemaphoreType.DMA((3,)),
        ],
        compiler_params=params(),
        name="owner",
    )(
        own,
        own_total,
        theirs,
        left_start,
        right_prev[0],
        traces,
        flag,
        left_kept,
        stay(right_root_prev[0]),
    )

    back = exchange(outgoing)
    theirs = swap(back)
    restored = jax.ShapeDtypeStruct((NB, 2048), BF16)
    restore_scratch = [
        pltpu.VMEM((NB * ROWS, 128), F32),
        pltpu.VMEM((NB, ROWS * 128), BF16),
        pltpu.SemaphoreType.DMA((4,)),
    ]
    halfway, right_use = pl.pallas_call(
        own_restore_kernel,
        out_shape=(restored, matrix),
        in_specs=[vmem()] * 3,
        out_specs=(hbm(), hbm()),
        scratch_shapes=restore_scratch + [pltpu.SemaphoreType.DMA],
        compiler_params=params(),
        cost_estimate=pl.CostEstimate(flops=NB * NB * ROWS * 256, bytes_accessed=4 * NB * ROWS * 128, transcendentals=0),
        name="own_restore",
    )(placed, back, right_root)
    update = pl.pallas_call(
        restore_kernel,
        out_shape=restored,
        in_specs=[vmem()] * 2 + [hbm()],
        out_specs=hbm(),
        scratch_shapes=restore_scratch,
        compiler_params=params(),
        input_output_aliases={2: 0},
        name="restore",
    )(placed, theirs, halfway)
    return (update, left_new[None], right_new[None], left_use[None], right_use[None])


def solution(mesh):
    placed = (
        P("dp", None, "fsdp"),
        P(),
        P(),
        P("fsdp", None, None),
        P("fsdp", None, None),
        P("fsdp", None, None),
        P("fsdp", None, None),
    )
    return jax.shard_map(
        local,
        mesh=mesh,
        in_specs=placed,
        out_specs=(
            P(None, "fsdp"),
            P("fsdp", None, None),
            P("fsdp", None, None),
            P("fsdp", None, None),
            P("fsdp", None, None),
        ),
        check_vma=False,
    )
```

```python
import functools

import jax
import jax.numpy as jnp
from jax import lax
from jax.experimental import pallas as pl
from jax.experimental.pallas import tpu as pltpu
from jax.sharding import PartitionSpec as P

BLK = 512
NB = 128
ROWS = 8
EPS = 0.001
F32 = jnp.float32
BF16 = jnp.bfloat16
VMEM_LIMIT = 24 * 1024 * 1024


def one_hot(held):
    block = lax.broadcasted_iota(jnp.int32, (NB, NB), 0)
    return jnp.where(block == held, 1.0, 0.0)


def to_slots(order, value_ref, rows_ref):
    half = lax.axis_index("dp")
    for row in range(4):
        columns = pl.ds(segment_column(2 * row, half), 256)
        pair = jnp.dot(order, value_ref[:, columns], preferred_element_type=F32)
        rows_ref[pl.ds(2 * row, NB, stride=ROWS), :] = pair[:, :128]
        rows_ref[pl.ds(2 * row + 1, NB, stride=ROWS), :] = pair[:, 128:]


def segment_column(part, half):
    return pl.multiple_of((part // 2) * BLK + half * 256 + (part % 2) * 128, 128)


def own_order_kernel(held_hbm, mine_hbm, rows_ref, placed_ref, order_ref, held_ref, mine_ref, sems):
    load_order = pltpu.make_async_copy(held_hbm, held_ref, sems.at[0])
    load = pltpu.make_async_copy(mine_hbm, mine_ref, sems.at[1])
    load_order.start()
    load.start()
    load_order.wait()
    placed = one_hot(held_ref[...])
    placed_ref[...] = placed.astype(BF16)
    order = placed.T.astype(BF16)
    order_ref[...] = order
    load.wait()
    to_slots(order, mine_ref, rows_ref)


def send_order_kernel(order_ref, own_ref, theirs_ref, out_ref, rows_ref):
    to_slots(order_ref[...], theirs_ref, rows_ref)
    out_ref[...] = (rows_ref[...] + own_ref[...]).astype(BF16)


def unpack_half(message_ref, rows_ref, write):
    rows_ref[...] = message_ref[...].astype(F32)
    total = jnp.zeros((8, 128), F32)
    for q in range(2):
        part = rows_ref[pl.ds(q, BLK, stride=2), :]
        write(q, part.astype(BF16))
        total = total + jnp.sum((part * part).reshape(BLK // 8, 8, 128), axis=0)
    return total


def diagonal(matrix_ref):
    total = jnp.zeros((8, 128), F32)
    for start in range(0, BLK, 128):
        block = matrix_ref[start : start + 128, start : start + 128]
        row = lax.broadcasted_iota(jnp.int32, (128, 128), 0)
        column = lax.broadcasted_iota(jnp.int32, (128, 128), 1)
        total = total + jnp.sum(jnp.where(row == column, block, 0.0).reshape(16, 8, 128), axis=0)
    return total


def own_unpack_kernel(
    mine_ref, left_prev, right_prev, left_root_hbm, held_hbm, refresh_hbm,
    grad_ref, total_ref, left_ref, traces_ref, flag_ref, kept_ref, rows_ref, held_ref, refresh_ref, sems,
):
    kept = pltpu.make_async_copy(left_root_hbm, kept_ref, sems.at[2])
    kept.start()
    loads = [
        pltpu.make_async_copy(held_hbm, held_ref, sems.at[0]),
        pltpu.make_async_copy(refresh_hbm, refresh_ref, sems.at[1]),
    ]
    for load in loads:
        load.start()

    def write(q, part):
        grad_ref[:, q * 128 : (q + 1) * 128] = part

    total_ref[...] = unpack_half(mine_ref, rows_ref, write)
    left_ref[...] = left_prev[...] + outer(grad_ref[...])
    traces_ref[0] = diagonal(left_prev)
    traces_ref[1] = diagonal(right_prev)
    for load in loads:
        load.wait()
    held = held_ref[lax.axis_index("fsdp")]
    refreshed = refresh_ref[0] == held
    for i in range(1, refresh_ref.shape[0]):
        refreshed = refreshed | (refresh_ref[i] == held)
    flag_ref[...] = jnp.full(flag_ref.shape, jnp.where(refreshed, 1.0, 0.0), F32)
    kept.wait()


def outer(value):
    return lax.dot_general(value, value, (((1,), (1,)), ((), ())), preferred_element_type=F32)


def inner(value):
    return lax.dot_general(value, value, (((0,), (0,)), ((), ())), preferred_element_type=F32)


def restore_half(placed_ref, message_ref, out_hbm, half, rows_ref, whole_ref, sems):
    placed = placed_ref[...]
    rows_ref[...] = message_ref[...].astype(F32)
    copies = []
    for row in range(4):
        pieces = [rows_ref[pl.ds(2 * row + q, NB, stride=ROWS), :].astype(BF16) for q in range(2)]
        whole_ref[:, row * 256 : (row + 1) * 256] = jnp.dot(
            placed, jnp.concatenate(pieces, axis=1), preferred_element_type=F32
        ).astype(BF16)
        columns = pl.ds(segment_column(2 * row, half), 256)
        source = whole_ref.at[:, row * 256 : (row + 1) * 256]
        copies.append(pltpu.make_async_copy(source, out_hbm.at[:, columns], sems.at[row]))
        copies[row].start()
    for copy in copies:
        copy.wait()


def own_restore_kernel(placed_ref, mine_ref, root_ref, out_hbm, root_hbm, rows_ref, whole_ref, sems, root_sem):
    store = pltpu.make_async_copy(root_ref, root_hbm, root_sem)
    store.start()
    restore_half(placed_ref, mine_ref, out_hbm, lax.axis_index("dp"), rows_ref, whole_ref, sems)
    store.wait()


def restore_kernel(placed_ref, theirs_ref, half_hbm, out_hbm, rows_ref, whole_ref, sems):
    del half_hbm
    restore_half(placed_ref, theirs_ref, out_hbm, 1 - lax.axis_index("dp"), rows_ref, whole_ref, sems)


def split(value):
    high = value.astype(BF16)
    return high, (value - high.astype(F32)).astype(BF16)


def store_split(ref, rows, value):
    ref[0, rows, :], ref[1, rows, :] = split(value)


def store_high(ref, rows, value):
    ref[0, rows, :] = value.astype(BF16)


def product(left_ref, right_ref):
    return (
        product_high(left_ref, right_ref)
        + jnp.dot(left_ref[0], right_ref[1], preferred_element_type=F32)
        + jnp.dot(left_ref[1], right_ref[0], preferred_element_type=F32)
    )


def product_high(left_ref, right_ref):
    return jnp.dot(left_ref[0], right_ref[0], preferred_element_type=F32)


CHUNK = 64


def add_diagonal(start, value, amount):
    block = start // 128 * 128
    row = lax.broadcasted_iota(jnp.int32, (CHUNK, 128), 0) + (start - block)
    column = lax.broadcasted_iota(jnp.int32, (CHUNK, 128), 1)
    touched = value[:, block : block + 128] + jnp.where(row == column, amount, 0.0)
    parts = [value[:, :block], touched, value[:, block + 128 :]]
    return jnp.concatenate([part for part in parts if part.shape[1]], axis=1)


ONE_PASS_ENERGY = 256.0


def newton(sides, traces, store, product, use, finish):
    scales, inverses, energies = [], [], []

    def shifted(i, start):
        return add_diagonal(start, sides[i][0][start : start + CHUNK, :] * inverses[i], EPS * inverses[i] - 1.0)

    def shift(i, factor_ref, x_ref, y_ref, z_ref, part_ref, root_ref):
        scale = (traces[i] + BLK * EPS) * (1.0 / BLK)
        inverses.append(1.0 / scale)
        scales.append(lax.rsqrt(jnp.sqrt(scale)))
        for start in range(0, BLK, CHUNK):
            store(x_ref, slice(start, start + CHUNK), shifted(i, start))

    def square(i, factor_ref, x_ref, y_ref, z_ref, part_ref, root_ref):
        value = product(x_ref, x_ref)
        energy = jnp.zeros((8, BLK), F32)
        for start in range(0, BLK, CHUNK):
            rows = slice(start, start + CHUNK)
            first, second = shifted(i, start), value[rows, :]
            energy = energy + jnp.sum((second * second).reshape(CHUNK // 8, 8, BLK), axis=0)
            part = first - second * 0.125
            part_ref[rows, :] = part
            store(y_ref, rows, part * -0.5)
            store(z_ref, rows, first * 0.75 - second * 0.25)
        energies.append(jnp.sum(energy, keepdims=True))

    def quartic(i, factor_ref, x_ref, y_ref, z_ref, part_ref, root_ref):
        value = product(y_ref, y_ref)
        for start in range(0, BLK, CHUNK):
            rows = slice(start, start + CHUNK)
            part, fourth = part_ref[rows, :], value[rows, :]
            part_ref[rows, :] = part + fourth
            store(x_ref, rows, fourth - part)

    def last(i, factor_ref, x_ref, y_ref, z_ref, part_ref, root_ref):
        value = product(x_ref, z_ref)
        for start in range(0, BLK, CHUNK):
            rows = slice(start, start + CHUNK)
            beside = (part_ref[rows, :] + value[rows, :]) * (scales[i] * -0.25)
            root = add_diagonal(start, beside, scales[i])
            root_ref[rows, :] = root
            use(i, rows, root, beside)
        finish(i)

    for step in (shift, square, quartic, last):
        for i, side in enumerate(sides):
            step(i, *side)
    return jnp.maximum(*energies), scales[0]


def owner_kernel(
    own_ref, own_total_ref, theirs_ref, left_start, right_prev, traces_ref, flag_ref, left_kept, right_root_prev,
    out_ref, left_out, right_out, left_root_out, right_r,
    rows_ref, grad_ref, left_f, right_f, left_r,
    left_x, left_y, left_z, left_p, right_x, right_y, right_z, right_p, left_use, right_use, in_sem, out_sems,
):
    half = lax.axis_index("dp")
    stores = [
        pltpu.make_async_copy(source, target, out_sems.at[i])
        for i, (source, target) in enumerate(
            ((left_f, left_out), (right_f, right_out), (left_r, left_root_out))
        )
    ]

    def columns(which, q):
        return pl.ds(pl.multiple_of(which * 256 + q * 128, 128), 128)

    def factors():
        parts = []

        def write(q, part):
            grad_ref[:, columns(1 - half, q)] = part
            parts.append(part)

        energy = jnp.sum(own_total_ref[...] + unpack_half(theirs_ref, rows_ref, write), keepdims=True)
        for q in range(2):
            grad_ref[:, columns(half, q)] = own_ref[:, q * 128 : (q + 1) * 128]
        left_f[...] = left_start[...] + outer(jnp.concatenate(parts, axis=1))
        stores[0].start()
        right_f[...] = right_prev[...] + inner(grad_ref[...])
        stores[1].start()
        return energy

    def use(i, rows, root, beside):
        if i == 0:
            left_use[0, rows, :] = beside.astype(BF16)
        else:
            right_use[rows, :] = root.astype(BF16)

    def finish(i):
        if i == 0:
            stores[2].start()

    def send(grad_energy, left_scale):
        grad = grad_ref[...]
        half_way = jnp.dot(left_use[0], grad, preferred_element_type=F32)
        if left_scale is None:
            half_way = half_way + jnp.dot(left_use[1], grad, preferred_element_type=F32)
        else:
            half_way = half_way + left_scale * grad.astype(F32)
        half_way = half_way.astype(BF16)
        total = jnp.zeros((8, 256), F32)
        for which in (half, 1 - half):
            span = pl.ds(pl.multiple_of(which * 256, 256), 256)
            raw = jnp.dot(half_way, right_use[:, span], preferred_element_type=F32)
            total = total + jnp.sum((raw * raw).reshape(BLK // 8, 8, 256), axis=0)
            if which is half:
                left_p[:, 0:256] = raw
        graft = jnp.sqrt(grad_energy) / jnp.sqrt(jnp.sum(total, keepdims=True) + 1e-06)
        for q in range(2):
            rows_ref[pl.ds(q, BLK, stride=2), :] = left_p[:, q * 128 : (q + 1) * 128] * graft
        out_ref[...] = rows_ref[...].astype(BF16)

    refreshed = flag_ref[0, 0] > 0.5

    @pl.when(refreshed)
    def _():
        grad_energy = factors()
        traces = [jnp.sum(traces_ref[i], keepdims=True) + grad_energy for i in range(2)]
        sides = (
            (left_f, left_x, left_y, left_z, left_p, left_r),
            (right_f, right_x, right_y, right_z, right_p, right_r),
        )
        energy, left_scale = newton(sides, traces, store_high, product_high, use, finish)
        send(grad_energy, left_scale)

        @pl.when(jnp.logical_not(energy[0, 0] <= ONE_PASS_ENERGY))
        def _():
            stores[2].wait()
            _, left_scale = newton(sides, traces, store_split, product, use, finish)
            send(grad_energy, left_scale)

    @pl.when(jnp.logical_not(refreshed))
    def _():
        load = pltpu.make_async_copy(right_root_prev, right_r, in_sem)
        load.start()
        pltpu.make_async_copy(left_kept, left_root_out, out_sems.at[2]).start()
        grad_energy = factors()
        for start in range(0, BLK, CHUNK):
            rows = slice(start, start + CHUNK)
            store_split(left_use, rows, left_kept[rows, :])
        load.wait()
        for start in range(0, BLK, CHUNK):
            rows = slice(start, start + CHUNK)
            right_use[rows, :] = right_r[rows, :].astype(BF16)
        send(grad_energy, None)

    for store in stores:
        store.wait()


def vmem():
    return pl.BlockSpec(memory_space=pltpu.VMEM)


def hbm():
    return pl.BlockSpec(memory_space=pltpu.HBM)


def stay(value):
    return pltpu.with_memory_space_constraint(value, pltpu.HBM)


def params(limit=VMEM_LIMIT):
    return pltpu.CompilerParams(vmem_limit_bytes=limit)


def swap(value):
    return lax.ppermute(value, "dp", [(0, 1), (1, 0)])


def exchange(messages):
    moved = lax.all_to_all(messages.reshape(NB, ROWS, 128), "fsdp", split_axis=0, concat_axis=0, tiled=True)
    return moved.reshape(NB * ROWS, 128)


def local(grad_parts, held_block, refresh, left_prev, right_prev, left_root_prev, right_root_prev):
    mine = grad_parts[0]
    held_row = held_block.reshape(1, NB)
    message = jax.ShapeDtypeStruct((NB * ROWS, 128), BF16)
    matrix = jax.ShapeDtypeStruct((BLK, BLK), F32)

    theirs = swap(mine)
    own, placed, order = pl.pallas_call(
        own_order_kernel,
        out_shape=(jax.ShapeDtypeStruct((NB * ROWS, 128), F32),) + 2 * (jax.ShapeDtypeStruct((NB, NB), BF16),),
        in_specs=[hbm(), hbm()],
        out_specs=(vmem(),) * 3,
        scratch_shapes=[
            pltpu.VMEM((1, NB), jnp.int32),
            pltpu.VMEM((NB, 2048), BF16),
            pltpu.SemaphoreType.DMA((2,)),
        ],
        compiler_params=params(),
        cost_estimate=pl.CostEstimate(flops=NB * NB * ROWS * 256, bytes_accessed=8 * NB * ROWS * 128, transcendentals=0),
        name="own_order",
    )(stay(held_row), stay(mine))
    ordered = pl.pallas_call(
        send_order_kernel,
        out_shape=message,
        in_specs=[vmem()] * 3,
        out_specs=vmem(),
        scratch_shapes=[pltpu.VMEM((NB * ROWS, 128), F32)],
        compiler_params=params(),
        name="send_order",
    )(order, own, theirs)
    got = exchange(ordered)

    theirs = swap(got)
    own, own_total, left_start, traces, flag, left_kept = pl.pallas_call(
        own_unpack_kernel,
        out_shape=(
            jax.ShapeDtypeStruct((BLK, 256), BF16),
            jax.ShapeDtypeStruct((8, 128), F32),
            matrix,
            jax.ShapeDtypeStruct((2, 8, 128), F32),
            jax.ShapeDtypeStruct((8, 128), F32),
            matrix,
        ),
        in_specs=[vmem()] * 3 + [hbm()] * 3,
        out_specs=(vmem(),) * 6,
        scratch_shapes=[
            pltpu.VMEM((NB * ROWS, 128), F32),
            pltpu.SMEM((NB,), jnp.int32),
            pltpu.SMEM(refresh.shape, jnp.int32),
            pltpu.SemaphoreType.DMA((3,)),
        ],
        compiler_params=params(),
        cost_estimate=pl.CostEstimate(flops=BLK * BLK * 512, bytes_accessed=8 * BLK * BLK, transcendentals=0),
        name="own_unpack",
    )(got, left_prev[0], right_prev[0], stay(left_root_prev[0]), stay(held_block), stay(refresh))
    outgoing, left_new, right_new, left_use, right_root = pl.pallas_call(
        owner_kernel,
        out_shape=(message, matrix, matrix, matrix, matrix),
        in_specs=[vmem()] * 8 + [hbm()],
        out_specs=(vmem(),) + (hbm(),) * 3 + (vmem(),),
        scratch_shapes=[pltpu.VMEM((NB * ROWS, 128), F32), pltpu.VMEM((BLK, BLK), BF16)]
        + 3 * [pltpu.VMEM((BLK, BLK), F32)]
        + 2 * (3 * [pltpu.VMEM((2, BLK, BLK), BF16)] + [pltpu.VMEM((BLK, BLK), F32)])
        + [
            pltpu.VMEM((2, BLK, BLK), BF16),
            pltpu.VMEM((BLK, BLK), BF16),
            pltpu.SemaphoreType.DMA,
            pltpu.SemaphoreType.DMA((3,)),
        ],
        compiler_params=params(),
        name="owner",
    )(
        own,
        own_total,
        theirs,
        left_start,
        right_prev[0],
        traces,
        flag,
        left_kept,
        stay(right_root_prev[0]),
    )

    back = exchange(outgoing)
    theirs = swap(back)
    restored = jax.ShapeDtypeStruct((NB, 2048), BF16)
    restore_scratch = [
        pltpu.VMEM((NB * ROWS, 128), F32),
        pltpu.VMEM((NB, ROWS * 128), BF16),
        pltpu.SemaphoreType.DMA((4,)),
    ]
    halfway, right_use = pl.pallas_call(
        own_restore_kernel,
        out_shape=(restored, matrix),
        in_specs=[vmem()] * 3,
        out_specs=(hbm(), hbm()),
        scratch_shapes=restore_scratch + [pltpu.SemaphoreType.DMA],
        compiler_params=params(),
        cost_estimate=pl.CostEstimate(flops=NB * NB * ROWS * 256, bytes_accessed=4 * NB * ROWS * 128, transcendentals=0),
        name="own_restore",
    )(placed, back, right_root)
    update = pl.pallas_call(
        restore_kernel,
        out_shape=restored,
        in_specs=[vmem()] * 2 + [hbm()],
        out_specs=hbm(),
        scratch_shapes=restore_scratch,
        compiler_params=params(),
        input_output_aliases={2: 0},
        name="restore",
    )(placed, theirs, halfway)
    return (update, left_new[None], right_new[None], left_use[None], right_use[None])


def solution(mesh):
    placed = (
        P("dp", None, "fsdp"),
        P(),
        P(),
        P("fsdp", None, None),
        P("fsdp", None, None),
        P("fsdp", None, None),
        P("fsdp", None, None),
    )
    return jax.shard_map(
        local,
        mesh=mesh,
        in_specs=placed,
        out_specs=(
            P(None, "fsdp"),
            P("fsdp", None, None),
            P("fsdp", None, None),
            P("fsdp", None, None),
            P("fsdp", None, None),
        ),
        check_vma=False,
    )
```

```python
import functools

import jax
import jax.numpy as jnp
from jax import lax
from jax.experimental import pallas as pl
from jax.experimental.pallas import tpu as pltpu
from jax.sharding import PartitionSpec as P

BLK = 512
NB = 128
ROWS = 8
EPS = 0.001
F32 = jnp.float32
BF16 = jnp.bfloat16
VMEM_LIMIT = 24 * 1024 * 1024


def one_hot(held):
    block = lax.broadcasted_iota(jnp.int32, (NB, NB), 0)
    return jnp.where(block == held, 1.0, 0.0)


def to_slots(order, value_ref, rows_ref):
    half = lax.axis_index("dp")
    for row in range(4):
        columns = pl.ds(segment_column(2 * row, half), 256)
        pair = jnp.dot(order, value_ref[:, columns], preferred_element_type=F32)
        rows_ref[pl.ds(2 * row, NB, stride=ROWS), :] = pair[:, :128]
        rows_ref[pl.ds(2 * row + 1, NB, stride=ROWS), :] = pair[:, 128:]


def segment_column(part, half):
    return pl.multiple_of((part // 2) * BLK + half * 256 + (part % 2) * 128, 128)


def own_order_kernel(held_hbm, mine_hbm, rows_ref, placed_ref, order_ref, held_ref, mine_ref, sems):
    load_order = pltpu.make_async_copy(held_hbm, held_ref, sems.at[0])
    load = pltpu.make_async_copy(mine_hbm, mine_ref, sems.at[1])
    load_order.start()
    load.start()
    load_order.wait()
    placed = one_hot(held_ref[...])
    placed_ref[...] = placed.astype(BF16)
    order = placed.T.astype(BF16)
    order_ref[...] = order
    load.wait()
    to_slots(order, mine_ref, rows_ref)


def send_order_kernel(order_ref, own_ref, theirs_ref, out_ref, rows_ref):
    to_slots(order_ref[...], theirs_ref, rows_ref)
    out_ref[...] = (rows_ref[...] + own_ref[...]).astype(BF16)


def unpack_half(message_ref, rows_ref, write):
    rows_ref[...] = message_ref[...].astype(F32)
    total = jnp.zeros((8, 128), F32)
    for q in range(2):
        part = rows_ref[pl.ds(q, BLK, stride=2), :]
        write(q, part.astype(BF16))
        total = total + jnp.sum((part * part).reshape(BLK // 8, 8, 128), axis=0)
    return total


def diagonal(matrix_ref):
    total = jnp.zeros((8, 128), F32)
    for start in range(0, BLK, 128):
        block = matrix_ref[start : start + 128, start : start + 128]
        row = lax.broadcasted_iota(jnp.int32, (128, 128), 0)
        column = lax.broadcasted_iota(jnp.int32, (128, 128), 1)
        total = total + jnp.sum(jnp.where(row == column, block, 0.0).reshape(16, 8, 128), axis=0)
    return total


def own_unpack_kernel(
    mine_ref, left_prev, right_prev, left_root_hbm, held_hbm, refresh_hbm,
    grad_ref, total_ref, left_ref, traces_ref, flag_ref, kept_ref, rows_ref, held_ref, refresh_ref, sems,
):
    kept = pltpu.make_async_copy(left_root_hbm, kept_ref, sems.at[2])
    kept.start()
    loads = [
        pltpu.make_async_copy(held_hbm, held_ref, sems.at[0]),
        pltpu.make_async_copy(refresh_hbm, refresh_ref, sems.at[1]),
    ]
    for load in loads:
        load.start()

    def write(q, part):
        grad_ref[:, q * 128 : (q + 1) * 128] = part

    total_ref[...] = unpack_half(mine_ref, rows_ref, write)
    left_ref[...] = left_prev[...] + outer(grad_ref[...])
    traces_ref[0] = diagonal(left_prev)
    traces_ref[1] = diagonal(right_prev)
    for load in loads:
        load.wait()
    held = held_ref[lax.axis_index("fsdp")]
    refreshed = refresh_ref[0] == held
    for i in range(1, refresh_ref.shape[0]):
        refreshed = refreshed | (refresh_ref[i] == held)
    flag_ref[...] = jnp.full(flag_ref.shape, jnp.where(refreshed, 1.0, 0.0), F32)
    kept.wait()


def outer(value):
    return lax.dot_general(value, value, (((1,), (1,)), ((), ())), preferred_element_type=F32)


def inner(value):
    return lax.dot_general(value, value, (((0,), (0,)), ((), ())), preferred_element_type=F32)


def restore_half(placed_ref, message_ref, out_hbm, half, rows_ref, whole_ref, sems):
    placed = placed_ref[...]
    rows_ref[...] = message_ref[...].astype(F32)
    copies = []
    for row in range(4):
        pieces = [rows_ref[pl.ds(2 * row + q, NB, stride=ROWS), :].astype(BF16) for q in range(2)]
        whole_ref[:, row * 256 : (row + 1) * 256] = jnp.dot(
            placed, jnp.concatenate(pieces, axis=1), preferred_element_type=F32
        ).astype(BF16)
        columns = pl.ds(segment_column(2 * row, half), 256)
        source = whole_ref.at[:, row * 256 : (row + 1) * 256]
        copies.append(pltpu.make_async_copy(source, out_hbm.at[:, columns], sems.at[row]))
        copies[row].start()
    for copy in copies:
        copy.wait()


def own_restore_kernel(placed_ref, mine_ref, root_ref, out_hbm, root_hbm, rows_ref, whole_ref, sems, root_sem):
    store = pltpu.make_async_copy(root_ref, root_hbm, root_sem)
    store.start()
    restore_half(placed_ref, mine_ref, out_hbm, lax.axis_index("dp"), rows_ref, whole_ref, sems)
    store.wait()


def restore_kernel(placed_ref, theirs_ref, half_hbm, out_hbm, rows_ref, whole_ref, sems):
    del half_hbm
    restore_half(placed_ref, theirs_ref, out_hbm, 1 - lax.axis_index("dp"), rows_ref, whole_ref, sems)


def split(value):
    high = value.astype(BF16)
    return high, (value - high.astype(F32)).astype(BF16)


def store_split(ref, rows, value):
    ref[0, rows, :], ref[1, rows, :] = split(value)


def store_high(ref, rows, value):
    ref[0, rows, :] = value.astype(BF16)


def product(left_ref, right_ref):
    return (
        product_high(left_ref, right_ref)
        + jnp.dot(left_ref[0], right_ref[1], preferred_element_type=F32)
        + jnp.dot(left_ref[1], right_ref[0], preferred_element_type=F32)
    )


def product_high(left_ref, right_ref):
    return jnp.dot(left_ref[0], right_ref[0], preferred_element_type=F32)


CHUNK = 32


def add_diagonal(start, value, amount):
    block = start // 128 * 128
    row = lax.broadcasted_iota(jnp.int32, (CHUNK, 128), 0) + (start - block)
    column = lax.broadcasted_iota(jnp.int32, (CHUNK, 128), 1)
    touched = value[:, block : block + 128] + jnp.where(row == column, amount, 0.0)
    parts = [value[:, :block], touched, value[:, block + 128 :]]
    return jnp.concatenate([part for part in parts if part.shape[1]], axis=1)


ONE_PASS_ENERGY = 256.0


def newton(sides, traces, store, product, use, finish):
    scales, inverses, energies = [], [], []

    def shifted(i, start):
        return add_diagonal(start, sides[i][0][start : start + CHUNK, :] * inverses[i], EPS * inverses[i] - 1.0)

    def shift(i, factor_ref, x_ref, y_ref, z_ref, part_ref, root_ref):
        scale = (traces[i] + BLK * EPS) * (1.0 / BLK)
        inverses.append(1.0 / scale)
        scales.append(lax.rsqrt(jnp.sqrt(scale)))
        for start in range(0, BLK, CHUNK):
            store(x_ref, slice(start, start + CHUNK), shifted(i, start))

    def square(i, factor_ref, x_ref, y_ref, z_ref, part_ref, root_ref):
        value = product(x_ref, x_ref)
        energy = jnp.zeros((8, BLK), F32)
        for start in range(0, BLK, CHUNK):
            rows = slice(start, start + CHUNK)
            first, second = shifted(i, start), value[rows, :]
            energy = energy + jnp.sum((second * second).reshape(CHUNK // 8, 8, BLK), axis=0)
            part = first - second * 0.125
            part_ref[rows, :] = part
            store(y_ref, rows, part * -0.5)
            store(z_ref, rows, first * 0.75 - second * 0.25)
        energies.append(jnp.sum(energy, keepdims=True))

    def quartic(i, factor_ref, x_ref, y_ref, z_ref, part_ref, root_ref):
        value = product(y_ref, y_ref)
        for start in range(0, BLK, CHUNK):
            rows = slice(start, start + CHUNK)
            part, fourth = part_ref[rows, :], value[rows, :]
            part_ref[rows, :] = part + fourth
            store(x_ref, rows, fourth - part)

    def last(i, factor_ref, x_ref, y_ref, z_ref, part_ref, root_ref):
        value = product(x_ref, z_ref)
        for start in range(0, BLK, CHUNK):
            rows = slice(start, start + CHUNK)
            beside = (part_ref[rows, :] + value[rows, :]) * (scales[i] * -0.25)
            root = add_diagonal(start, beside, scales[i])
            root_ref[rows, :] = root
            use(i, rows, root, beside)
        finish(i)

    for step in (shift, square, quartic, last):
        for i, side in enumerate(sides):
            step(i, *side)
    return jnp.maximum(*energies), scales[0]


def owner_kernel(
    own_ref, own_total_ref, theirs_ref, left_start, right_prev, traces_ref, flag_ref, left_kept, right_root_prev,
    out_ref, left_out, right_out, left_root_out, right_r,
    rows_ref, grad_ref, left_f, right_f, left_r,
    left_x, left_y, left_z, left_p, right_x, right_y, right_z, right_p, left_use, right_use, in_sem, out_sems,
):
    half = lax.axis_index("dp")
    stores = [
        pltpu.make_async_copy(source, target, out_sems.at[i])
        for i, (source, target) in enumerate(
            ((left_f, left_out), (right_f, right_out), (left_r, left_root_out))
        )
    ]

    def columns(which, q):
        return pl.ds(pl.multiple_of(which * 256 + q * 128, 128), 128)

    def factors():
        parts = []

        def write(q, part):
            grad_ref[:, columns(1 - half, q)] = part
            parts.append(part)

        energy = jnp.sum(own_total_ref[...] + unpack_half(theirs_ref, rows_ref, write), keepdims=True)
        for q in range(2):
            grad_ref[:, columns(half, q)] = own_ref[:, q * 128 : (q + 1) * 128]
        left_f[...] = left_start[...] + outer(jnp.concatenate(parts, axis=1))
        stores[0].start()
        right_f[...] = right_prev[...] + inner(grad_ref[...])
        stores[1].start()
        return energy

    def use(i, rows, root, beside):
        if i == 0:
            left_use[0, rows, :] = beside.astype(BF16)
        else:
            right_use[rows, :] = root.astype(BF16)

    def finish(i):
        if i == 0:
            stores[2].start()

    def send(grad_energy, left_scale):
        grad = grad_ref[...]
        half_way = jnp.dot(left_use[0], grad, preferred_element_type=F32)
        if left_scale is None:
            half_way = half_way + jnp.dot(left_use[1], grad, preferred_element_type=F32)
        else:
            half_way = half_way + left_scale * grad.astype(F32)
        half_way = half_way.astype(BF16)
        total = jnp.zeros((8, 256), F32)
        for which in (half, 1 - half):
            span = pl.ds(pl.multiple_of(which * 256, 256), 256)
            raw = jnp.dot(half_way, right_use[:, span], preferred_element_type=F32)
            total = total + jnp.sum((raw * raw).reshape(BLK // 8, 8, 256), axis=0)
            if which is half:
                left_p[:, 0:256] = raw
        graft = jnp.sqrt(grad_energy) / jnp.sqrt(jnp.sum(total, keepdims=True) + 1e-06)
        for q in range(2):
            rows_ref[pl.ds(q, BLK, stride=2), :] = left_p[:, q * 128 : (q + 1) * 128] * graft
        out_ref[...] = rows_ref[...].astype(BF16)

    refreshed = flag_ref[0, 0] > 0.5

    @pl.when(refreshed)
    def _():
        grad_energy = factors()
        traces = [jnp.sum(traces_ref[i], keepdims=True) + grad_energy for i in range(2)]
        sides = (
            (left_f, left_x, left_y, left_z, left_p, left_r),
            (right_f, right_x, right_y, right_z, right_p, right_r),
        )
        energy, left_scale = newton(sides, traces, store_high, product_high, use, finish)
        send(grad_energy, left_scale)

        @pl.when(jnp.logical_not(energy[0, 0] <= ONE_PASS_ENERGY))
        def _():
            stores[2].wait()
            _, left_scale = newton(sides, traces, store_split, product, use, finish)
            send(grad_energy, left_scale)

    @pl.when(jnp.logical_not(refreshed))
    def _():
        load = pltpu.make_async_copy(right_root_prev, right_r, in_sem)
        load.start()
        pltpu.make_async_copy(left_kept, left_root_out, out_sems.at[2]).start()
        grad_energy = factors()
        for start in range(0, BLK, CHUNK):
            rows = slice(start, start + CHUNK)
            store_split(left_use, rows, left_kept[rows, :])
        load.wait()
        for start in range(0, BLK, CHUNK):
            rows = slice(start, start + CHUNK)
            right_use[rows, :] = right_r[rows, :].astype(BF16)
        send(grad_energy, None)

    for store in stores:
        store.wait()


def vmem():
    return pl.BlockSpec(memory_space=pltpu.VMEM)


def hbm():
    return pl.BlockSpec(memory_space=pltpu.HBM)


def stay(value):
    return pltpu.with_memory_space_constraint(value, pltpu.HBM)


def params(limit=VMEM_LIMIT):
    return pltpu.CompilerParams(vmem_limit_bytes=limit)


def swap(value):
    return lax.ppermute(value, "dp", [(0, 1), (1, 0)])


def exchange(messages):
    moved = lax.all_to_all(messages.reshape(NB, ROWS, 128), "fsdp", split_axis=0, concat_axis=0, tiled=True)
    return moved.reshape(NB * ROWS, 128)


def local(grad_parts, held_block, refresh, left_prev, right_prev, left_root_prev, right_root_prev):
    mine = grad_parts[0]
    held_row = held_block.reshape(1, NB)
    message = jax.ShapeDtypeStruct((NB * ROWS, 128), BF16)
    matrix = jax.ShapeDtypeStruct((BLK, BLK), F32)

    theirs = swap(mine)
    own, placed, order = pl.pallas_call(
        own_order_kernel,
        out_shape=(jax.ShapeDtypeStruct((NB * ROWS, 128), F32),) + 2 * (jax.ShapeDtypeStruct((NB, NB), BF16),),
        in_specs=[hbm(), hbm()],
        out_specs=(vmem(),) * 3,
        scratch_shapes=[
            pltpu.VMEM((1, NB), jnp.int32),
            pltpu.VMEM((NB, 2048), BF16),
            pltpu.SemaphoreType.DMA((2,)),
        ],
        compiler_params=params(),
        cost_estimate=pl.CostEstimate(flops=NB * NB * ROWS * 256, bytes_accessed=8 * NB * ROWS * 128, transcendentals=0),
        name="own_order",
    )(stay(held_row), stay(mine))
    ordered = pl.pallas_call(
        send_order_kernel,
        out_shape=message,
        in_specs=[vmem()] * 3,
        out_specs=vmem(),
        scratch_shapes=[pltpu.VMEM((NB * ROWS, 128), F32)],
        compiler_params=params(),
        name="send_order",
    )(order, own, theirs)
    got = exchange(ordered)

    theirs = swap(got)
    own, own_total, left_start, traces, flag, left_kept = pl.pallas_call(
        own_unpack_kernel,
        out_shape=(
            jax.ShapeDtypeStruct((BLK, 256), BF16),
            jax.ShapeDtypeStruct((8, 128), F32),
            matrix,
            jax.ShapeDtypeStruct((2, 8, 128), F32),
            jax.ShapeDtypeStruct((8, 128), F32),
            matrix,
        ),
        in_specs=[vmem()] * 3 + [hbm()] * 3,
        out_specs=(vmem(),) * 6,
        scratch_shapes=[
            pltpu.VMEM((NB * ROWS, 128), F32),
            pltpu.SMEM((NB,), jnp.int32),
            pltpu.SMEM(refresh.shape, jnp.int32),
            pltpu.SemaphoreType.DMA((3,)),
        ],
        compiler_params=params(),
        cost_estimate=pl.CostEstimate(flops=BLK * BLK * 512, bytes_accessed=8 * BLK * BLK, transcendentals=0),
        name="own_unpack",
    )(got, left_prev[0], right_prev[0], stay(left_root_prev[0]), stay(held_block), stay(refresh))
    outgoing, left_new, right_new, left_use, right_root = pl.pallas_call(
        owner_kernel,
        out_shape=(message, matrix, matrix, matrix, matrix),
        in_specs=[vmem()] * 8 + [hbm()],
        out_specs=(vmem(),) + (hbm(),) * 3 + (vmem(),),
        scratch_shapes=[pltpu.VMEM((NB * ROWS, 128), F32), pltpu.VMEM((BLK, BLK), BF16)]
        + 3 * [pltpu.VMEM((BLK, BLK), F32)]
        + 2 * (3 * [pltpu.VMEM((2, BLK, BLK), BF16)] + [pltpu.VMEM((BLK, BLK), F32)])
        + [
            pltpu.VMEM((2, BLK, BLK), BF16),
            pltpu.VMEM((BLK, BLK), BF16),
            pltpu.SemaphoreType.DMA,
            pltpu.SemaphoreType.DMA((3,)),
        ],
        compiler_params=params(),
        name="owner",
    )(
        own,
        own_total,
        theirs,
        left_start,
        right_prev[0],
        traces,
        flag,
        left_kept,
        stay(right_root_prev[0]),
    )

    back = exchange(outgoing)
    theirs = swap(back)
    restored = jax.ShapeDtypeStruct((NB, 2048), BF16)
    restore_scratch = [
        pltpu.VMEM((NB * ROWS, 128), F32),
        pltpu.VMEM((NB, ROWS * 128), BF16),
        pltpu.SemaphoreType.DMA((4,)),
    ]
    halfway, right_use = pl.pallas_call(
        own_restore_kernel,
        out_shape=(restored, matrix),
        in_specs=[vmem()] * 3,
        out_specs=(hbm(), hbm()),
        scratch_shapes=restore_scratch + [pltpu.SemaphoreType.DMA],
        compiler_params=params(),
        cost_estimate=pl.CostEstimate(flops=NB * NB * ROWS * 256, bytes_accessed=4 * NB * ROWS * 128, transcendentals=0),
        name="own_restore",
    )(placed, back, right_root)
    update = pl.pallas_call(
        restore_kernel,
        out_shape=restored,
        in_specs=[vmem()] * 2 + [hbm()],
        out_specs=hbm(),
        scratch_shapes=restore_scratch,
        compiler_params=params(),
        input_output_aliases={2: 0},
        name="restore",
    )(placed, theirs, halfway)
    return (update, left_new[None], right_new[None], left_use[None], right_use[None])


def solution(mesh):
    placed = (
        P("dp", None, "fsdp"),
        P(),
        P(),
        P("fsdp", None, None),
        P("fsdp", None, None),
        P("fsdp", None, None),
        P("fsdp", None, None),
    )
    return jax.shard_map(
        local,
        mesh=mesh,
        in_specs=placed,
        out_specs=(
            P(None, "fsdp"),
            P("fsdp", None, None),
            P("fsdp", None, None),
            P("fsdp", None, None),
            P("fsdp", None, None),
        ),
        check_vma=False,
    )
```
